512 devices in a mesh: rep: 16 (over x, z_hi, core), fsdp: 32 (over z_lo, y).
Axes of the slice: x: 4, y: 4, z: 16 (z_hi: 2, z_lo: 8; z = z_hi * 8 + z_lo), core: 2. Of those that a mesh axis runs over, the one named last changes fastest.
Arguments:
- tokens_in: bfloat16 [16, 1536, 2048], P('rep', 'fsdp'), may hold values from -6 to 6
- cotangent: bfloat16 [16, 1536, 2048], P('rep', 'fsdp'), may hold values from -6 to 6
- up_weight: bfloat16 [2048, 8192], P(None, 'fsdp'), may hold values from -0.125 to 0.125
- down_weight: bfloat16 [8192, 2048], P('fsdp'), may hold values from -0.0625 to 0.0625
- up_moment: float32 [2048, 8192], P('rep', 'fsdp'), may hold values from -4 to 4
- down_moment: float32 [8192, 2048], P('fsdp', 'rep'), may hold values from -4 to 4
Outputs:
- new_up: bfloat16 [2048, 8192], P(None, 'fsdp')
- new_down: bfloat16 [8192, 2048], P('fsdp')
- new_up_moment: float32 [2048, 8192], P('rep', 'fsdp')
- new_down_moment: float32 [8192, 2048], P('fsdp', 'rep')
The draws below stay inside these ranges and needn't reach their ends.
All inputs are finite; a program needn't handle non-finite values.
Results may differ from the reference program's by a relative error of at most 0.023.
Values may be sent and summed in bfloat16 or wider, within the bound.
A program may use at most 64 MiB of HBM per device.

```python
import jax
import jax.numpy as jnp
from jax import lax

D = 2048
FF = 8192
REPLICAS = 16
TOKENS_REP = 1536
N_REP = 16


def level_of(stream_key, extent, shards, least, top_value):
    factor_of, own = 1.0, jax.random.fold_in(stream_key, 6)
    for axis_at, shards_of in shards:
        heights = jnp.exp(jax.random.uniform(jax.random.fold_in(own, axis_at), (shards_of,), jnp.float32, least / len(shards), top_value / len(shards)))
        factor_of = factor_of * jnp.repeat(heights, extent[axis_at] // shards_of).reshape([-1 if axis == axis_at else 1 for axis in range(len(extent))])
    return factor_of


def gaussian(rng, dims, spread, bound, cuts=(), dtype=jnp.bfloat16):
    array = spread * jax.random.normal(rng, dims, jnp.float32)
    if cuts:
        array = array * level_of(rng, dims, cuts, -0.22, 0.18)
    return jnp.clip(array, -bound, bound).astype(dtype)


def setup_inputs(seed: int = 0) -> dict:
    seeds = jax.random.split(jax.random.key(seed), 7)
    return {
        "tokens_in": gaussian(seeds[0], (REPLICAS, TOKENS_REP, D), 1.0, 6.0, ((0, 16), (1, 32))),
        "cotangent": gaussian(seeds[1], (REPLICAS, TOKENS_REP, D), 1.0, 6.0, ((0, 16), (1, 32))),
        "up_weight": gaussian(seeds[2], (D, FF), D ** -0.5, 0.125, ((1, 32),)),
        "down_weight": gaussian(seeds[3], (FF, D), FF ** -0.5, 0.0625, ((0, 32),)),
        "up_moment": gaussian(seeds[4], (D, FF), 0.5, 4.0, ((0, 16), (1, 32)), jnp.float32),
        "down_moment": gaussian(seeds[5], (FF, D), 0.5, 4.0, ((0, 32), (1, 16)), jnp.float32),
    }


inner_rate = 0.3
outer_rate = 0.7
momentum_factor = 0.9


def replica_deltas(rows_in, rows_back, up_weight, down_weight):
    pre = jnp.dot(rows_in, up_weight, preferred_element_type=jnp.float32)
    act = jax.nn.silu(pre).astype(jnp.bfloat16)
    back = jnp.dot(rows_back, down_weight.T, preferred_element_type=jnp.float32)
    sig = jax.nn.sigmoid(pre)
    dpre = (back * sig * (1.0 + pre * (1.0 - sig))).astype(jnp.bfloat16)
    grad_down = jnp.dot(act.T, rows_back, preferred_element_type=jnp.float32)
    grad_up = jnp.dot(rows_in.T, dpre, preferred_element_type=jnp.float32)
    return (inner_rate * grad_up).astype(jnp.bfloat16), (inner_rate * grad_down).astype(jnp.bfloat16)


def reference(tokens_in, cotangent, up_weight, down_weight, up_moment, down_moment):
    def accumulate(carry, pair):
        delta_up, delta_down = replica_deltas(pair[0], pair[1], up_weight, down_weight)
        return (carry[0] + delta_up.astype(jnp.float32), carry[1] + delta_down.astype(jnp.float32)), None

    start = (jnp.zeros(up_weight.shape, jnp.float32), jnp.zeros(down_weight.shape, jnp.float32))
    totals, _ = lax.scan(accumulate, start, (tokens_in, cotangent))
    mean_up = totals[0] / N_REP
    mean_down = totals[1] / N_REP
    new_up_moment = momentum_factor * up_moment + mean_up
    new_down_moment = momentum_factor * down_moment + mean_down
    new_up = (up_weight.astype(jnp.float32) - outer_rate * (mean_up + momentum_factor * new_up_moment)).astype(jnp.bfloat16)
    new_down = (down_weight.astype(jnp.float32) - outer_rate * (mean_down + momentum_factor * new_down_moment)).astype(jnp.bfloat16)
    return new_up, new_down, new_up_moment, new_down_moment
```

```python
import functools

import jax
import jax.numpy as jnp
from jax import lax
from jax.experimental import pallas as pl
from jax.experimental.pallas import tpu as pltpu
from jax.sharding import PartitionSpec as P

inner_rate = 0.3
outer_rate = 0.7
momentum_factor = 0.9

MESH = pl.DeviceIdType.MESH
F32 = jnp.float32
BF16 = jnp.bfloat16

ROWS = 48
SLAB = 4 * ROWS
D = 2048
FL = 256
Q4 = D // 4


def device(x, zhi, core, zlo, y):
    return {"rep": (x * 2 + zhi) * 2 + core, "fsdp": zlo * 4 + y}


def outer_round(
    tok, cot, up, down, mu, md,
    o_up, o_dn, o_mu, o_md,
    X, G, Wu, Wd, accU, accD, dT, aT, sb, rb, ys, yr, cs, cb, zr, us, ds, muv, mdv,
    ld, sxz, rxz, sgz, rgz, sxy, rxy, sgy, rgy, sxc, rxc, sgc, rgc, sw, rw,
    sx, rx, sy, ry, sc, rc, sz, rz, sA, rA, sC, rC,
):
    rep = lax.axis_index("rep")
    fs = lax.axis_index("fsdp")
    x, zhi, core = rep // 4, (rep // 2) % 2, rep % 2
    zlo, y = fs // 4, fs % 4
    z = zhi * 8 + zlo
    sgn = 1 - 2 * core

    def at_z(zz):
        zz = (zz + 32) % 16
        return device(x, zz // 8, core, zz % 8, y)

    def at_x(xx):
        return device((xx + 8) % 4, zhi, core, zlo, y)

    to_long = at_z(z + sgn)
    to_short = at_z(z - sgn)
    to_pair = device(x, zhi, core, zlo, y + 1 - 2 * (y % 2))
    to_slice = device(x, zhi, core, zlo, 3 - y)
    to_core = device(x, zhi, 1 - core, zlo, y)
    to_right = at_x(x + 1)
    to_left = at_x(x - 1)
    to_zhi = device(x, 1 - zhi, core, zlo, y)
    home = (y % 2) == core

    def local(src, dst, sem):
        return pltpu.make_async_copy(src, dst, sem)

    def remote(src, dst, ssem, rsem, to):
        return pltpu.make_async_remote_copy(
            src_ref=src, dst_ref=dst, send_sem=ssem, recv_sem=rsem,
            device_id=to, device_id_type=MESH,
        )

    def slot(buf, zi, yi, ci):
        return buf.at[pl.ds(zi * SLAB + (yi * 2 + ci) * ROWS, ROWS), :]

    share_row = pl.multiple_of(rep * 128, 128)
    loads = [
        local(tok, slot(X, 0, 0, 0), ld.at[0]),
        local(cot, slot(G, 0, 0, 0), ld.at[1]),
        local(up.at[pl.ds(share_row, 128), :], us, ld.at[2]),
        local(down.at[:, pl.ds(share_row, 128)], ds, ld.at[3]),
        local(mu, muv, ld.at[4]),
        local(md, mdv, ld.at[5]),
    ]
    for c in loads:
        c.start()

    barrier = pltpu.get_barrier_semaphore()
    everyone = (to_long, to_short, to_pair, to_slice, to_core, to_right, to_left, to_zhi)
    for other in everyone:
        pl.semaphore_signal(barrier, inc=1, device_id=other, device_id_type=MESH)
    loads[0].wait()
    loads[1].wait()
    pl.semaphore_wait(barrier, len(everyone))

    sent = []

    def go(copy):
        copy.start()
        sent.append(copy)

    def x_z(src_zi, dst_zi, to):
        return remote(slot(X, src_zi, 0, 0), slot(X, dst_zi, 0, 0), sxz.at[dst_zi], rxz.at[dst_zi], to)

    def g_z(src_zi, dst_zi, yi, to):
        return remote(
            slot(G, src_zi, yi, 0), slot(G, dst_zi, yi, 0), sgz.at[dst_zi, yi], rgz.at[dst_zi, yi], to
        )

    def x_y(zi):
        return remote(slot(X, zi, 0, 0), slot(X, zi, 1, 0), sxy.at[zi], rxy.at[zi], to_pair)

    def g_y():
        return remote(slot(G, 0, 0, 0), slot(G, 0, 1, 0), sgy.at[0], rgy.at[0], to_pair)

    def x_c(zi, yi):
        return remote(slot(X, zi, yi, 0), slot(X, zi, yi, 1), sxc.at[zi, yi], rxc.at[zi, yi], to_core)

    def g_c(zi, yi):
        return remote(slot(G, zi, yi, 0), slot(G, zi, yi, 1), sgc.at[zi, yi], rgc.at[zi, yi], to_core)

    go(g_y())
    go(x_z(0, 1, to_long))
    go(x_z(0, 2, to_short))
    go(g_z(0, 1, 0, to_long))
    go(g_z(0, 2, 0, to_short))
    go(x_y(0))
    go(x_c(0, 0))
    go(g_c(0, 0))

    w_send = [
        remote(up, Wu, sw.at[0], rw.at[0], to_slice),
        remote(down, Wd, sw.at[1], rw.at[1], to_slice),
    ]
    w_local = [local(up, Wu, ld.at[6]), local(down, Wd, ld.at[7])]

    @pl.when(home)
    def _():
        for c in w_send + w_local:
            c.start()

    g_y().wait_recv()
    go(g_z(0, 1, 1, to_long))
    go(g_z(0, 2, 1, to_short))
    go(g_c(0, 1))
    x_y(0).wait_recv()
    go(x_c(0, 1))

    def arrived_x(zi, onward, to):
        x_z(0, zi, to_long).wait_recv()
        if onward:
            go(x_z(zi, zi + 2, to))
        go(x_y(zi))
        go(x_c(zi, 0))

    def arrived_g(zi, yi, onward, to):
        g_z(0, zi, yi, to_long).wait_recv()
        if onward:
            go(g_z(zi, zi + 2, yi, to))
        go(g_c(zi, yi))

    def arrived_pair(zi):
        x_y(zi).wait_recv()
        go(x_c(zi, 1))

    for k in (1, 2, 3):
        long, short = 2 * k - 1, 2 * k
        arrived_x(long, True, to_long)
        arrived_x(short, k < 3, to_short)
        arrived_g(long, 0, True, to_long)
        arrived_g(short, 0, k < 3, to_short)
        arrived_pair(long)
        arrived_pair(short)
        arrived_g(long, 1, True, to_long)
        arrived_g(short, 1, k < 3, to_short)

    def from_core(zi):
        for yi in (0, 1):
            x_c(zi, yi).wait_recv()
            g_c(zi, yi).wait_recv()

    def middle(row, n):
        rows = pl.ds(row, n)
        pre = jnp.dot(X[rows, :], Wu[...], preferred_element_type=F32)
        back = lax.dot_general(G[rows, :], Wd[...], (((1,), (1,)), ((), ())), preferred_element_type=F32)
        s = jax.nn.sigmoid(pre)
        act = pre * s
        dpre = back * s * (1.0 + pre * (1.0 - s))
        dT[:, :n] = dpre.T.astype(BF16)
        aT[:, :n] = act.T.astype(BF16)

    def grads(row, n, first):
        rows = pl.ds(row, n)

        @pl.loop(0, D // 256)
        def _(j):
            cols = pl.ds(pl.multiple_of(j * 256, 256), 256)
            du = jnp.dot(dT[:, :n], X[rows, cols], preferred_element_type=F32)
            dd = jnp.dot(aT[:, :n], G[rows, cols], preferred_element_type=F32)
            accU[:, cols] = du if first else accU[:, cols] + du
            accD[:, cols] = dd if first else accD[:, cols] + dd

    @pl.when(home)
    def _():
        for c in w_local:
            c.wait()

    @pl.when(jnp.logical_not(home))
    def _():
        for c in w_send:
            c.wait_recv()

    from_core(0)
    middle(0, SLAB)
    grads(0, SLAB, True)
    for k in (1, 2):
        from_core(2 * k - 1)
        from_core(2 * k)
        middle((2 * k - 1) * SLAB, 2 * SLAB)
        grads((2 * k - 1) * SLAB, 2 * SLAB, False)

    arrived_x(7, False, to_long)
    from_core(5)
    from_core(6)
    middle(5 * SLAB, 2 * SLAB)
    grads(5 * SLAB, 2 * SLAB, False)
    arrived_g(7, 0, False, to_long)
    arrived_pair(7)
    arrived_g(7, 1, False, to_long)
    from_core(7)
    middle(7 * SLAB, SLAB)

    last = pl.ds(7 * SLAB, SLAB)

    def quarter(step):
        return pl.ds(pl.multiple_of(((x + step) % 4) * Q4, Q4), Q4)

    def total_up(cols):
        return accU[:, cols] + jnp.dot(dT[:, :SLAB], X[last, cols], preferred_element_type=F32)

    def total_dn(cols):
        return accD[:, cols] + jnp.dot(aT[:, :SLAB], G[last, cols], preferred_element_type=F32)

    def x_sum(i):
        return remote(sb.at[i], rb.at[i], sx.at[i], rx.at[i], to_right if i % 2 == 0 else to_left)

    sb[0] = total_up(quarter(2)).astype(BF16)
    go(x_sum(0))
    sb[1] = total_dn(quarter(2)).astype(BF16)
    go(x_sum(1))
    sb[2] = total_dn(quarter(1)).astype(BF16)
    go(x_sum(2))
    sb[3] = total_up(quarter(3)).astype(BF16)
    go(x_sum(3))
    accU[:, quarter(1)] = total_up(quarter(1))
    accD[:, quarter(3)] = total_dn(quarter(3))
    x_sum(0).wait_recv()
    sb[4] = (accU[:, quarter(1)] + rb[0].astype(F32)).astype(BF16)
    go(x_sum(4))
    x_sum(1).wait_recv()
    sb[5] = (accD[:, quarter(3)] + rb[1].astype(F32)).astype(BF16)
    go(x_sum(5))
    accU[:, quarter(0)] = total_up(quarter(0))
    accD[:, quarter(0)] = total_dn(quarter(0))
    for i in (2, 3, 4, 5):
        x_sum(i).wait_recv()

    def part(a, off, width):
        cols = pl.ds(pl.multiple_of(x * Q4 + off, 128), width)
        here = pl.ds(pl.multiple_of(off, 128), width)
        if a == 0:
            return accU[:, cols] + rb[3, :, here].astype(F32) + rb[4, :, here].astype(F32)
        return accD[:, cols] + rb[2, :, here].astype(F32) + rb[5, :, here].astype(F32)

    def y_sum(a):
        return remote(ys.at[a], yr.at[a], sy.at[a], ry.at[a], to_slice)

    def c_sum(h, a):
        return remote(cs.at[h, a], cb.at[h, a], sc.at[h, a], rc.at[h, a], to_core)

    @pl.when(jnp.logical_not(home))
    def _():
        for a in (0, 1):
            ys[a] = part(a, 0, Q4).astype(BF16)
            y_sum(a).start()
        for a in (0, 1):
            for h in (0, 1):
                c_sum(h, a).wait_recv()
        for a in (0, 1):
            y_sum(a).wait_send()

    @pl.when(home)
    def _():
        for a in (0, 1):
            y_sum(a).wait_recv()
            for h in (0, 1):
                theirs = pl.multiple_of(h * 256 + (1 - core) * 128, 128)
                mine = pl.multiple_of(h * 256 + core * 128, 128)
                cs[h, a] = (part(a, theirs, 128) + yr[a, :, pl.ds(theirs, 128)].astype(F32)).astype(BF16)
                c_sum(h, a).start()
                cb[h, a] = (part(a, mine, 128) + yr[a, :, pl.ds(mine, 128)].astype(F32)).astype(BF16)
        for a in (0, 1):
            for h in (0, 1):
                c_sum(h, a).wait_send()
        for c in w_send:
            c.wait_send()

    def z_sum(a):
        return remote(cb.at[1 - zhi, a], zr.at[a], sz.at[a], rz.at[a], to_zhi)

    for a in (0, 1):
        go(z_sum(a))
    for c in loads[2:]:
        c.wait()

    replicas = 16

    def spot(a, xx, zz, cc):
        at = pl.ds(pl.multiple_of(((xx * 2 + zz) * 2 + cc) * 128, 128), 128)
        return o_up.at[at, :] if a == 0 else o_dn.at[:, at]

    z_sum(0).wait_recv()
    mean = (cb[zhi, 0].astype(F32) + zr[0].astype(F32)).T * (inner_rate / replicas)
    moment = momentum_factor * muv[...] + mean
    o_mu[...] = moment
    o_up[pl.ds(share_row, 128), :] = (
        us[...].astype(F32) - outer_rate * (mean + momentum_factor * moment)
    ).astype(BF16)

    def a_z(a):
        return remote(spot(a, x, zhi, core), spot(a, x, zhi, core), sA.at[1, 0, a], rA.at[1, 0, a], to_zhi)

    def z_in(a):
        return remote(spot(a, x, zhi, core), spot(a, x, 1 - zhi, core), sA.at[1, 0, a], rA.at[1, 0, a], to_zhi)

    go(a_z(0))
    z_sum(1).wait_recv()
    mean = (cb[zhi, 1].astype(F32) + zr[1].astype(F32)) * (inner_rate / replicas)
    moment = momentum_factor * mdv[...] + mean
    o_md[...] = moment
    o_dn[:, pl.ds(share_row, 128)] = (
        ds[...].astype(F32) - outer_rate * (mean + momentum_factor * moment)
    ).astype(BF16)
    go(a_z(1))

    back_by = {0: 0, 1: 1, 2: 2, 3: -1}

    def hold(a, q, j):
        return spot(a, (x - back_by[j] + 4) % 4, (zhi + q) % 2, core)

    def a_x(a, q, j, dst_j, to):
        return remote(hold(a, q, j), hold(a, q, j), sA.at[q, dst_j, a], rA.at[q, dst_j, a], to)

    def x_in(a, q, j):
        return remote(hold(a, q, j), hold(a, q, j), sA.at[q, j, a], rA.at[q, j, a], to_right)

    def a_c(a, q, j):
        return remote(hold(a, q, j), hold(a, q, j), sC.at[q, j, a], rC.at[q, j, a], to_core)

    def c_in(a, q, j):
        there = spot(a, (x - back_by[j] + 4) % 4, (zhi + q) % 2, 1 - core)
        return remote(there, there, sC.at[q, j, a], rC.at[q, j, a], to_core)

    for q in (0, 1):
        if q == 1:
            for a in (0, 1):
                z_in(a).wait_recv()
                go(a_x(a, 1, 0, 1, to_right))
                go(a_x(a, 1, 0, 3, to_left))
                go(a_c(a, 1, 0))
        else:
            for a in (0, 1):
                go(a_x(a, 0, 0, 1, to_right))
                go(a_x(a, 0, 0, 3, to_left))
                go(a_c(a, 0, 0))
        x_in(0, q, 1).wait_recv()
        go(a_x(0, q, 1, 2, to_right))
        go(a_c(0, q, 1))
        x_in(1, q, 3).wait_recv()
        go(a_x(1, q, 3, 2, to_left))
        go(a_c(1, q, 3))
        x_in(1, q, 1).wait_recv()
        go(a_c(1, q, 1))
        x_in(0, q, 3).wait_recv()
        go(a_c(0, q, 3))
        for a in (0, 1):
            x_in(a, q, 2).wait_recv()
            go(a_c(a, q, 2))
    for q in (0, 1):
        for j in (0, 1, 2, 3):
            for a in (0, 1):
                c_in(a, q, j).wait_recv()
    for c in sent:
        c.wait_send()


def local(tokens_in, cotangent, up_weight, down_weight, up_moment, down_moment):
    dma = pltpu.SemaphoreType.DMA
    vmem = pltpu.VMEM
    return pl.pallas_call(
        outer_round,
        out_shape=(
            jax.ShapeDtypeStruct(up_weight.shape, BF16),
            jax.ShapeDtypeStruct(down_weight.shape, BF16),
            jax.ShapeDtypeStruct(up_moment.shape, F32),
            jax.ShapeDtypeStruct(down_moment.shape, F32),
        ),
        in_specs=[pl.BlockSpec(memory_space=pl.ANY)] * 6,
        out_specs=[pl.BlockSpec(memory_space=pltpu.VMEM)] * 4,
        scratch_shapes=[
            vmem((8 * SLAB, D), BF16), vmem((8 * SLAB, D), BF16),
            vmem((D, FL), BF16), vmem((FL, D), BF16),
            vmem((FL, D), F32), vmem((FL, D), F32),
            vmem((FL, 2 * SLAB), BF16), vmem((FL, 2 * SLAB), BF16),
            vmem((6, FL, Q4), BF16), vmem((6, FL, Q4), BF16),
            vmem((2, FL, Q4), BF16), vmem((2, FL, Q4), BF16),
            vmem((2, 2, FL, 128), BF16), vmem((2, 2, FL, 128), BF16),
            vmem((2, FL, 128), BF16),
            vmem((128, FL), BF16), vmem((FL, 128), BF16),
            vmem((128, FL), F32), vmem((FL, 128), F32),
            dma((8,)),
            dma((8,)), dma((8,)), dma((8, 2)), dma((8, 2)), dma((8,)), dma((8,)), dma((1,)), dma((1,)),
            dma((8, 2)), dma((8, 2)), dma((8, 2)), dma((8, 2)), dma((2,)), dma((2,)),
            dma((6,)), dma((6,)), dma((2,)), dma((2,)), dma((2, 2)), dma((2, 2)), dma((2,)), dma((2,)),
            dma((2, 4, 2)), dma((2, 4, 2)), dma((2, 4, 2)), dma((2, 4, 2)),
        ],
        compiler_params=pltpu.CompilerParams(
            collective_id=0, has_side_effects=True, vmem_limit_bytes=48 << 20
        ),
        name="outer_round",
    )(tokens_in[0], cotangent[0], up_weight, down_weight, up_moment, down_moment)


def solution(mesh):
    return jax.shard_map(
        local,
        mesh=mesh,
        in_specs=(
            P("rep", "fsdp", None),
            P("rep", "fsdp", None),
            P(None, "fsdp"),
            P("fsdp", None),
            P("rep", "fsdp"),
            P("fsdp", "rep"),
        ),
        out_specs=(P(None, "fsdp"), P("fsdp", None), P("rep", "fsdp"), P("fsdp", "rep")),
        check_vma=False,
    )
```

```python
import functools

import jax
import jax.numpy as jnp
from jax import lax
from jax.experimental import pallas as pl
from jax.experimental.pallas import tpu as pltpu
from jax.sharding import PartitionSpec as P

inner_rate = 0.3
outer_rate = 0.7
momentum_factor = 0.9

MESH = pl.DeviceIdType.MESH
F32 = jnp.float32
BF16 = jnp.bfloat16

ROWS = 48
SLAB = 4 * ROWS
D = 2048
FL = 256
Q4 = D // 4


def device(x, zhi, core, zlo, y):
    return {"rep": (x * 2 + zhi) * 2 + core, "fsdp": zlo * 4 + y}


def outer_round(
    tok, cot, up, down, mu, md,
    o_up, o_dn, o_mu, o_md,
    X, G, Wu, Wd, accU, accD, dT, aT, sb, rb, ys, yr, cs, cb, zr, us, ds, muv, mdv,
    ld, sxz, rxz, sgz, rgz, sxy, rxy, sgy, rgy, sxc, rxc, sgc, rgc, sw, rw,
    sx, rx, sy, ry, sc, rc, sz, rz, sA, rA, sC, rC,
):
    rep = lax.axis_index("rep")
    fs = lax.axis_index("fsdp")
    x, zhi, core = rep // 4, (rep // 2) % 2, rep % 2
    zlo, y = fs // 4, fs % 4
    z = zhi * 8 + zlo
    sgn = 1 - 2 * core

    def at_z(zz):
        zz = (zz + 32) % 16
        return device(x, zz // 8, core, zz % 8, y)

    def at_x(xx):
        return device((xx + 8) % 4, zhi, core, zlo, y)

    to_long = at_z(z + sgn)
    to_short = at_z(z - sgn)
    to_pair = device(x, zhi, core, zlo, y + 1 - 2 * (y % 2))
    to_slice = device(x, zhi, core, zlo, 3 - y)
    to_core = device(x, zhi, 1 - core, zlo, y)
    to_right = at_x(x + 1)
    to_left = at_x(x - 1)
    to_zhi = device(x, 1 - zhi, core, zlo, y)
    home = (y % 2) == core

    def local(src, dst, sem):
        return pltpu.make_async_copy(src, dst, sem)

    def remote(src, dst, ssem, rsem, to):
        return pltpu.make_async_remote_copy(
            src_ref=src, dst_ref=dst, send_sem=ssem, recv_sem=rsem,
            device_id=to, device_id_type=MESH,
        )

    def slot(buf, zi, yi, ci):
        return buf.at[pl.ds(zi * SLAB + (yi * 2 + ci) * ROWS, ROWS), :]

    share_row = pl.multiple_of(rep * 128, 128)
    loads = [
        local(tok, slot(X, 0, 0, 0), ld.at[0]),
        local(cot, slot(G, 0, 0, 0), ld.at[1]),
        local(up.at[pl.ds(share_row, 128), :], us, ld.at[2]),
        local(down.at[:, pl.ds(share_row, 128)], ds, ld.at[3]),
        local(mu, muv, ld.at[4]),
        local(md, mdv, ld.at[5]),
    ]
    for c in loads:
        c.start()

    barrier = pltpu.get_barrier_semaphore()
    everyone = (to_long, to_short, to_pair, to_slice, to_core, to_right, to_left, to_zhi)
    for other in everyone:
        pl.semaphore_signal(barrier, inc=1, device_id=other, device_id_type=MESH)
    loads[0].wait()
    loads[1].wait()
    pl.semaphore_wait(barrier, len(everyone))

    sent = []

    def go(copy):
        copy.start()
        sent.append(copy)

    def x_z(src_zi, dst_zi, to):
        return remote(slot(X, src_zi, 0, 0), slot(X, dst_zi, 0, 0), sxz.at[dst_zi], rxz.at[dst_zi], to)

    def g_z(src_zi, dst_zi, yi, to):
        return remote(
            slot(G, src_zi, yi, 0), slot(G, dst_zi, yi, 0), sgz.at[dst_zi, yi], rgz.at[dst_zi, yi], to
        )

    def x_y(zi):
        return remote(slot(X, zi, 0, 0), slot(X, zi, 1, 0), sxy.at[zi], rxy.at[zi], to_pair)

    def g_y():
        return remote(slot(G, 0, 0, 0), slot(G, 0, 1, 0), sgy.at[0], rgy.at[0], to_pair)

    def x_c(zi, yi):
        return remote(slot(X, zi, yi, 0), slot(X, zi, yi, 1), sxc.at[zi, yi], rxc.at[zi, yi], to_core)

    def g_c(zi, yi):
        return remote(slot(G, zi, yi, 0), slot(G, zi, yi, 1), sgc.at[zi, yi], rgc.at[zi, yi], to_core)

    go(g_y())
    go(x_z(0, 1, to_long))
    go(x_z(0, 2, to_short))
    go(g_z(0, 1, 0, to_long))
    go(g_z(0, 2, 0, to_short))
    go(x_y(0))
    go(x_c(0, 0))
    go(g_c(0, 0))

    w_send = [
        remote(up, Wu, sw.at[0], rw.at[0], to_slice),
        remote(down, Wd, sw.at[1], rw.at[1], to_slice),
    ]
    w_local = [local(up, Wu, ld.at[6]), local(down, Wd, ld.at[7])]

    @pl.when(home)
    def _():
        for c in w_send + w_local:
            c.start()

    g_y().wait_recv()
    go(g_z(0, 1, 1, to_long))
    go(g_z(0, 2, 1, to_short))
    go(g_c(0, 1))
    x_y(0).wait_recv()
    go(x_c(0, 1))

    def arrived_x(zi, onward, to):
        x_z(0, zi, to_long).wait_recv()
        if onward:
            go(x_z(zi, zi + 2, to))
        go(x_y(zi))
        go(x_c(zi, 0))

    def arrived_g(zi, yi, onward, to):
        g_z(0, zi, yi, to_long).wait_recv()
        if onward:
            go(g_z(zi, zi + 2, yi, to))
        go(g_c(zi, yi))

    def arrived_pair(zi):
        x_y(zi).wait_recv()
        go(x_c(zi, 1))

    def from_core(zi):
        for yi in (0, 1):
            x_c(zi, yi).wait_recv()
            g_c(zi, yi).wait_recv()

    def middle(zi):
        rows = pl.ds(zi * SLAB, SLAB)
        pre = jnp.dot(X[rows, :], Wu[...], preferred_element_type=F32)
        back = lax.dot_general(G[rows, :], Wd[...], (((1,), (1,)), ((), ())), preferred_element_type=F32)
        s = jax.nn.sigmoid(pre)
        act = pre * s
        dpre = back * s * (1.0 + pre * (1.0 - s))
        dT[...] = dpre.T.astype(BF16)
        aT[...] = act.T.astype(BF16)

    def grads(zi):
        rows = pl.ds(zi * SLAB, SLAB)

        @pl.loop(0, D // 256)
        def _(j):
            cols = pl.ds(pl.multiple_of(j * 256, 256), 256)
            du = jnp.dot(dT[...], X[rows, cols], preferred_element_type=F32)
            dd = jnp.dot(aT[...], G[rows, cols], preferred_element_type=F32)
            accU[:, cols] = du if zi == 0 else accU[:, cols] + du
            accD[:, cols] = dd if zi == 0 else accD[:, cols] + dd

    def unit(zi):
        from_core(zi)
        middle(zi)
        grads(zi)

    for k in (1, 2, 3):
        long, short = 2 * k - 1, 2 * k
        arrived_x(long, True, to_long)
        arrived_x(short, k < 3, to_short)
        if k == 3:

            @pl.when(home)
            def _():
                for c in w_local:
                    c.wait()

            @pl.when(jnp.logical_not(home))
            def _():
                for c in w_send:
                    c.wait_recv()

            unit(0)
        arrived_g(long, 0, True, to_long)
        arrived_g(short, 0, k < 3, to_short)
        if k == 3:
            unit(1)
        arrived_pair(long)
        arrived_pair(short)
        if k == 3:
            unit(2)
        arrived_g(long, 1, True, to_long)
        arrived_g(short, 1, k < 3, to_short)
        if k == 3:
            unit(3)

    arrived_x(7, False, to_long)
    unit(4)
    arrived_g(7, 0, False, to_long)
    unit(5)
    arrived_pair(7)
    unit(6)
    arrived_g(7, 1, False, to_long)
    from_core(7)
    middle(7)

    last = pl.ds(7 * SLAB, SLAB)
    H4 = Q4 // 2
    half = (1 - zhi, zhi)

    def cols(step, i):
        return pl.ds(pl.multiple_of(((x + step) % 4) * Q4 + half[i] * H4, H4), H4)

    def total_up(at):
        return accU[:, at] + jnp.dot(dT[...], X[last, at], preferred_element_type=F32)

    def total_dn(at):
        return accD[:, at] + jnp.dot(aT[...], G[last, at], preferred_element_type=F32)

    def x_sum(i, n):
        return remote(
            sb.at[i, n], rb.at[i, n], sx.at[i, n], rx.at[i, n], to_right if n % 2 == 0 else to_left
        )

    def x_first(i):
        sb[i, 0] = total_up(cols(2, i)).astype(BF16)
        go(x_sum(i, 0))
        sb[i, 1] = total_dn(cols(2, i)).astype(BF16)
        go(x_sum(i, 1))
        sb[i, 2] = total_dn(cols(1, i)).astype(BF16)
        go(x_sum(i, 2))
        sb[i, 3] = total_up(cols(3, i)).astype(BF16)
        go(x_sum(i, 3))

    def x_rest(i):
        for a, step in ((0, 1), (1, 3), (0, 0), (1, 0)):
            if a == 0:
                accU[:, cols(step, i)] = total_up(cols(step, i))
            else:
                accD[:, cols(step, i)] = total_dn(cols(step, i))

    def x_relay(i):
        x_sum(i, 0).wait_recv()
        sb[i, 4] = (accU[:, cols(1, i)] + rb[i, 0].astype(F32)).astype(BF16)
        go(x_sum(i, 4))
        x_sum(i, 1).wait_recv()
        sb[i, 5] = (accD[:, cols(3, i)] + rb[i, 1].astype(F32)).astype(BF16)
        go(x_sum(i, 5))

    def part(i, a, off, width):
        at = pl.ds(pl.multiple_of(x * Q4 + half[i] * H4 + off, 128), width)
        here = pl.ds(pl.multiple_of(off, 128), width)
        if a == 0:
            return accU[:, at] + rb[i, 3, :, here].astype(F32) + rb[i, 4, :, here].astype(F32)
        return accD[:, at] + rb[i, 2, :, here].astype(F32) + rb[i, 5, :, here].astype(F32)

    def y_sum(i, a):
        return remote(ys.at[i, a], yr.at[i, a], sy.at[i, a], ry.at[i, a], to_slice)

    def c_sum(i, a):
        return remote(cs.at[i, a], cb.at[i, a], sc.at[i, a], rc.at[i, a], to_core)

    def y_out(i):
        for n in (2, 3, 4, 5):
            x_sum(i, n).wait_recv()

        @pl.when(jnp.logical_not(home))
        def _():
            for a in (0, 1):
                ys[i, a] = part(i, a, 0, H4).astype(BF16)
                y_sum(i, a).start()

    def y_in(i):
        @pl.when(jnp.logical_not(home))
        def _():
            for a in (0, 1):
                c_sum(i, a).wait_recv()
            for a in (0, 1):
                y_sum(i, a).wait_send()

        @pl.when(home)
        def _():
            for a in (0, 1):
                y_sum(i, a).wait_recv()
                theirs = pl.multiple_of((1 - core) * 128, 128)
                mine = pl.multiple_of(core * 128, 128)
                cs[i, a] = (part(i, a, theirs, 128) + yr[i, a, :, pl.ds(theirs, 128)].astype(F32)).astype(BF16)
                c_sum(i, a).start()
                cb[i, a] = (part(i, a, mine, 128) + yr[i, a, :, pl.ds(mine, 128)].astype(F32)).astype(BF16)
            for a in (0, 1):
                c_sum(i, a).wait_send()

    def z_sum(a):
        return remote(cb.at[0, a], zr.at[a], sz.at[a], rz.at[a], to_zhi)

    x_first(0)
    x_rest(0)
    x_relay(0)
    x_first(1)
    x_rest(1)
    y_out(0)
    x_relay(1)
    y_in(0)
    for a in (0, 1):
        go(z_sum(a))
    y_out(1)
    y_in(1)

    @pl.when(home)
    def _():
        for c in w_send:
            c.wait_send()

    for c in loads[2:]:
        c.wait()

    replicas = 16

    def spot(a, xx, zz, cc):
        at = pl.ds(pl.multiple_of(((xx * 2 + zz) * 2 + cc) * 128, 128), 128)
        return o_up.at[at, :] if a == 0 else o_dn.at[:, at]

    z_sum(0).wait_recv()
    mean = (cb[1, 0].astype(F32) + zr[0].astype(F32)).T * (inner_rate / replicas)
    moment = momentum_factor * muv[...] + mean
    o_mu[...] = moment
    o_up[pl.ds(share_row, 128), :] = (
        us[...].astype(F32) - outer_rate * (mean + momentum_factor * moment)
    ).astype(BF16)

    def a_z(a):
        return remote(spot(a, x, zhi, core), spot(a, x, zhi, core), sA.at[1, 0, a], rA.at[1, 0, a], to_zhi)

    def z_in(a):
        return remote(spot(a, x, zhi, core), spot(a, x, 1 - zhi, core), sA.at[1, 0, a], rA.at[1, 0, a], to_zhi)

    go(a_z(0))
    z_sum(1).wait_recv()
    mean = (cb[1, 1].astype(F32) + zr[1].astype(F32)) * (inner_rate / replicas)
    moment = momentum_factor * mdv[...] + mean
    o_md[...] = moment
    o_dn[:, pl.ds(share_row, 128)] = (
        ds[...].astype(F32) - outer_rate * (mean + momentum_factor * moment)
    ).astype(BF16)
    go(a_z(1))

    back_by = {0: 0, 1: 1, 2: 2, 3: -1}

    def hold(a, q, j):
        return spot(a, (x - back_by[j] + 4) % 4, (zhi + q) % 2, core)

    def a_x(a, q, j, dst_j, to):
        return remote(hold(a, q, j), hold(a, q, j), sA.at[q, dst_j, a], rA.at[q, dst_j, a], to)

    def x_in(a, q, j):
        return remote(hold(a, q, j), hold(a, q, j), sA.at[q, j, a], rA.at[q, j, a], to_right)

    def a_c(a, q, j):
        return remote(hold(a, q, j), hold(a, q, j), sC.at[q, j, a], rC.at[q, j, a], to_core)

    def c_in(a, q, j):
        there = spot(a, (x - back_by[j] + 4) % 4, (zhi + q) % 2, 1 - core)
        return remote(there, there, sC.at[q, j, a], rC.at[q, j, a], to_core)

    for q in (0, 1):
        if q == 1:
            for a in (0, 1):
                z_in(a).wait_recv()
                go(a_x(a, 1, 0, 1, to_right))
                go(a_x(a, 1, 0, 3, to_left))
                go(a_c(a, 1, 0))
        else:
            for a in (0, 1):
                go(a_x(a, 0, 0, 1, to_right))
                go(a_x(a, 0, 0, 3, to_left))
                go(a_c(a, 0, 0))
        x_in(0, q, 1).wait_recv()
        go(a_x(0, q, 1, 2, to_right))
        go(a_c(0, q, 1))
        x_in(1, q, 3).wait_recv()
        go(a_x(1, q, 3, 2, to_left))
        go(a_c(1, q, 3))
        x_in(1, q, 1).wait_recv()
        go(a_c(1, q, 1))
        x_in(0, q, 3).wait_recv()
        go(a_c(0, q, 3))
        for a in (0, 1):
            x_in(a, q, 2).wait_recv()
            go(a_c(a, q, 2))
    for q in (0, 1):
        for j in (0, 1, 2, 3):
            for a in (0, 1):
                c_in(a, q, j).wait_recv()
    for c in sent:
        c.wait_send()


def local(tokens_in, cotangent, up_weight, down_weight, up_moment, down_moment):
    dma = pltpu.SemaphoreType.DMA
    vmem = pltpu.VMEM
    return pl.pallas_call(
        outer_round,
        out_shape=(
            jax.ShapeDtypeStruct(up_weight.shape, BF16),
            jax.ShapeDtypeStruct(down_weight.shape, BF16),
            jax.ShapeDtypeStruct(up_moment.shape, F32),
            jax.ShapeDtypeStruct(down_moment.shape, F32),
        ),
        in_specs=[pl.BlockSpec(memory_space=pltpu.HBM)] * 6,
        out_specs=[pl.BlockSpec(memory_space=pltpu.VMEM)] * 4,
        scratch_shapes=[
            vmem((8 * SLAB, D), BF16), vmem((8 * SLAB, D), BF16),
            vmem((D, FL), BF16), vmem((FL, D), BF16),
            vmem((FL, D), F32), vmem((FL, D), F32),
            vmem((FL, SLAB), BF16), vmem((FL, SLAB), BF16),
            vmem((2, 6, FL, Q4 // 2), BF16), vmem((2, 6, FL, Q4 // 2), BF16),
            vmem((2, 2, FL, Q4 // 2), BF16), vmem((2, 2, FL, Q4 // 2), BF16),
            vmem((2, 2, FL, 128), BF16), vmem((2, 2, FL, 128), BF16),
            vmem((2, FL, 128), BF16),
            vmem((128, FL), BF16), vmem((FL, 128), BF16),
            vmem((128, FL), F32), vmem((FL, 128), F32),
            dma((8,)),
            dma((8,)), dma((8,)), dma((8, 2)), dma((8, 2)), dma((8,)), dma((8,)), dma((1,)), dma((1,)),
            dma((8, 2)), dma((8, 2)), dma((8, 2)), dma((8, 2)), dma((2,)), dma((2,)),
            dma((2, 6)), dma((2, 6)), dma((2, 2)), dma((2, 2)), dma((2, 2)), dma((2, 2)), dma((2,)), dma((2,)),
            dma((2, 4, 2)), dma((2, 4, 2)), dma((2, 4, 2)), dma((2, 4, 2)),
        ],
        compiler_params=pltpu.CompilerParams(
            collective_id=0, has_side_effects=True, vmem_limit_bytes=60 << 20
        ),
        name="outer_round",
    )(tokens_in[0], cotangent[0], up_weight, down_weight, up_moment, down_moment)


def solution(mesh):
    return jax.shard_map(
        local,
        mesh=mesh,
        in_specs=(
            P("rep", "fsdp", None),
            P("rep", "fsdp", None),
            P(None, "fsdp"),
            P("fsdp", None),
            P("rep", "fsdp"),
            P("fsdp", "rep"),
        ),
        out_specs=(P(None, "fsdp"), P("fsdp", None), P("rep", "fsdp"), P("fsdp", "rep")),
        check_vma=False,
    )
```

```python
import functools

import jax
import jax.numpy as jnp
from jax import lax
from jax.experimental import pallas as pl
from jax.experimental.pallas import tpu as pltpu
from jax.sharding import PartitionSpec as P

inner_rate = 0.3
outer_rate = 0.7
momentum_factor = 0.9

MESH = pl.DeviceIdType.MESH
F32 = jnp.float32
BF16 = jnp.bfloat16

ROWS = 48
SLAB = 4 * ROWS
D = 2048
FL = 256
Q4 = D // 4


def device(x, zhi, core, zlo, y):
    return {"rep": (x * 2 + zhi) * 2 + core, "fsdp": zlo * 4 + y}


def outer_round(
    tok, cot, up, down, mu, md,
    o_up, o_dn, o_mu, o_md,
    X, G, Wu, Wd, accU, accD, dT, aT, sb, rb, ys, yr, cs, cb, zr, us, ds, muv, mdv, W,
    ld, sxz, rxz, sgz, rgz, sxy, rxy, sgy, rgy, sxc, rxc, sgc, rgc, sw, rw,
    sx, rx, sy, ry, sc, rc, sz, rz, sA, rA, sC, rC,
):
    rep = lax.axis_index("rep")
    fs = lax.axis_index("fsdp")
    x, zhi, core = rep // 4, (rep // 2) % 2, rep % 2
    zlo, y = fs // 4, fs % 4
    z = zhi * 8 + zlo
    sgn = 1 - 2 * core

    def at_z(zz):
        zz = (zz + 32) % 16
        return device(x, zz // 8, core, zz % 8, y)

    def at_x(xx):
        return device((xx + 8) % 4, zhi, core, zlo, y)

    to_long = at_z(z + sgn)
    to_short = at_z(z - sgn)
    to_pair = device(x, zhi, core, zlo, y + 1 - 2 * (y % 2))
    to_slice = device(x, zhi, core, zlo, 3 - y)
    to_core = device(x, zhi, 1 - core, zlo, y)
    to_right = at_x(x + 1)
    to_left = at_x(x - 1)
    to_zhi = device(x, 1 - zhi, core, zlo, y)
    home = (y % 2) == core

    def local(src, dst, sem):
        return pltpu.make_async_copy(src, dst, sem)

    def remote(src, dst, ssem, rsem, to):
        return pltpu.make_async_remote_copy(
            src_ref=src, dst_ref=dst, send_sem=ssem, recv_sem=rsem,
            device_id=to, device_id_type=MESH,
        )

    def slot(buf, zi, yi, ci):
        return buf.at[pl.ds(zi * SLAB + (yi * 2 + ci) * ROWS, ROWS), :]

    share_row = pl.multiple_of(rep * 128, 128)
    loads = [
        local(tok, slot(X, 0, 0, 0), ld.at[0]),
        local(cot, slot(G, 0, 0, 0), ld.at[1]),
        local(up.at[pl.ds(share_row, 128), :], us, ld.at[2]),
        local(down.at[:, pl.ds(share_row, 128)], ds, ld.at[3]),
        local(mu, muv, ld.at[4]),
        local(md, mdv, ld.at[5]),
    ]
    for c in loads:
        c.start()

    barrier = pltpu.get_barrier_semaphore()
    everyone = (to_long, to_short, to_pair, to_slice, to_core, to_right, to_left, to_zhi)
    for other in everyone:
        pl.semaphore_signal(barrier, inc=1, device_id=other, device_id_type=MESH)
    loads[0].wait()
    loads[1].wait()
    pl.semaphore_wait(barrier, len(everyone))

    sent = []

    def go(copy):
        copy.start()
        sent.append(copy)

    def x_z(src_zi, dst_zi, to):
        return remote(slot(X, src_zi, 0, 0), slot(X, dst_zi, 0, 0), sxz.at[dst_zi], rxz.at[dst_zi], to)

    def g_z(src_zi, dst_zi, yi, to):
        return remote(
            slot(G, src_zi, yi, 0), slot(G, dst_zi, yi, 0), sgz.at[dst_zi, yi], rgz.at[dst_zi, yi], to
        )

    def x_y(zi):
        return remote(slot(X, zi, 0, 0), slot(X, zi, 1, 0), sxy.at[zi], rxy.at[zi], to_pair)

    def g_y():
        return remote(slot(G, 0, 0, 0), slot(G, 0, 1, 0), sgy.at[0], rgy.at[0], to_pair)

    def x_c(zi, yi):
        return remote(slot(X, zi, yi, 0), slot(X, zi, yi, 1), sxc.at[zi, yi], rxc.at[zi, yi], to_core)

    def g_c(zi, yi):
        return remote(slot(G, zi, yi, 0), slot(G, zi, yi, 1), sgc.at[zi, yi], rgc.at[zi, yi], to_core)

    go(g_y())
    go(x_z(0, 1, to_long))
    go(x_z(0, 2, to_short))
    go(g_z(0, 1, 0, to_long))
    go(g_z(0, 2, 0, to_short))
    go(x_y(0))
    go(x_c(0, 0))
    go(g_c(0, 0))

    w_send = [
        remote(up, Wu, sw.at[0], rw.at[0], to_slice),
        remote(down, Wd, sw.at[1], rw.at[1], to_slice),
    ]
    w_local = [local(up, Wu, sw.at[2]), local(down, Wd, sw.at[3])]

    @pl.when(home)
    def _():
        for c in w_send + w_local:
            c.start()

    g_y().wait_recv()
    go(g_z(0, 1, 1, to_long))
    go(g_z(0, 2, 1, to_short))
    go(g_c(0, 1))
    x_y(0).wait_recv()
    go(x_c(0, 1))

    def arrived_x(zi, onward, to):
        x_z(0, zi, to_long).wait_recv()
        if onward:
            go(x_z(zi, zi + 2, to))
        go(x_y(zi))
        go(x_c(zi, 0))

    def arrived_g(zi, yi, onward, to):
        g_z(0, zi, yi, to_long).wait_recv()
        if onward:
            go(g_z(zi, zi + 2, yi, to))
        go(g_c(zi, yi))

    def arrived_pair(zi):
        x_y(zi).wait_recv()
        go(x_c(zi, 1))

    def from_core(zi):
        for yi in (0, 1):
            x_c(zi, yi).wait_recv()
            g_c(zi, yi).wait_recv()

    def middle(zi):
        rows = pl.ds(zi * SLAB, SLAB)
        pre = jnp.dot(X[rows, :], Wu[...], preferred_element_type=F32)
        back = lax.dot_general(G[rows, :], Wd[...], (((1,), (1,)), ((), ())), preferred_element_type=F32)
        s = jax.nn.sigmoid(pre)
        act = pre * s
        dpre = back * s * (1.0 + pre * (1.0 - s))
        dT[...] = dpre.astype(BF16).T
        aT[...] = act.astype(BF16).T

    def grads(zi):
        rows = pl.ds(zi * SLAB, SLAB)

        @pl.loop(0, D // 256)
        def _(j):
            cols = pl.ds(pl.multiple_of(j * 256, 256), 256)
            du = jnp.dot(dT[...], X[rows, cols], preferred_element_type=F32)
            dd = jnp.dot(aT[...], G[rows, cols], preferred_element_type=F32)
            accU[:, cols] = du if zi == 0 else accU[:, cols] + du
            accD[:, cols] = dd if zi == 0 else accD[:, cols] + dd

    def unit(zi):
        from_core(zi)
        middle(zi)
        grads(zi)

    for k in (1, 2, 3):
        long, short = 2 * k - 1, 2 * k
        arrived_x(long, True, to_long)
        arrived_x(short, k < 3, to_short)
        if k == 3:
            unit(1)
        arrived_g(long, 0, True, to_long)
        arrived_g(short, 0, k < 3, to_short)
        if k == 3:
            unit(2)
        arrived_pair(long)
        arrived_pair(short)
        if k == 3:
            unit(3)
        arrived_g(long, 1, True, to_long)
        arrived_g(short, 1, k < 3, to_short)
        if k == 2:

            @pl.when(home)
            def _():
                for c in w_local:
                    c.wait()

            @pl.when(jnp.logical_not(home))
            def _():
                for c in w_send:
                    c.wait_recv()

            unit(0)
        if k == 3:
            unit(4)

    arrived_x(7, False, to_long)
    unit(5)
    arrived_g(7, 0, False, to_long)
    unit(6)
    arrived_pair(7)
    arrived_g(7, 1, False, to_long)
    from_core(7)
    middle(7)

    last = pl.ds(7 * SLAB, SLAB)
    H4 = Q4 // 2
    HR = FL // 2
    half = (1 - zhi, zhi)

    def hidden(m):
        return pl.ds(m * HR, HR)

    def cols(step, i):
        return pl.ds(pl.multiple_of(((x + step) % 4) * Q4 + half[i] * H4, H4), H4)

    def total_up(m, at):
        return accU[hidden(m), at] + jnp.dot(dT[hidden(m), :], X[last, at], preferred_element_type=F32)

    def total_dn(m, at):
        return accD[hidden(m), at] + jnp.dot(aT[hidden(m), :], G[last, at], preferred_element_type=F32)

    def x_sum(m, i, n):
        return remote(
            sb.at[m, i, n], rb.at[m, i, n], sx.at[m, i, n], rx.at[m, i, n],
            to_right if n % 2 == 0 else to_left,
        )

    def x_first(m, i):
        sb[m, i, 0] = total_up(m, cols(2, i)).astype(BF16)
        go(x_sum(m, i, 0))
        sb[m, i, 1] = total_dn(m, cols(2, i)).astype(BF16)
        go(x_sum(m, i, 1))
        sb[m, i, 2] = total_dn(m, cols(1, i)).astype(BF16)
        go(x_sum(m, i, 2))
        sb[m, i, 3] = total_up(m, cols(3, i)).astype(BF16)
        go(x_sum(m, i, 3))
        for step in (1, 0):
            accU[hidden(m), cols(step, i)] = total_up(m, cols(step, i))
        for step in (3, 0):
            accD[hidden(m), cols(step, i)] = total_dn(m, cols(step, i))

    def x_relay(m, i):
        x_sum(m, i, 0).wait_recv()
        sb[m, i, 4] = (accU[hidden(m), cols(1, i)] + rb[m, i, 0].astype(F32)).astype(BF16)
        go(x_sum(m, i, 4))
        x_sum(m, i, 1).wait_recv()
        sb[m, i, 5] = (accD[hidden(m), cols(3, i)] + rb[m, i, 1].astype(F32)).astype(BF16)
        go(x_sum(m, i, 5))

    def part(m, i, a, off, width):
        at = pl.ds(pl.multiple_of(x * Q4 + half[i] * H4 + off, 128), width)
        here = pl.ds(pl.multiple_of(off, 128), width)
        if a == 0:
            return accU[hidden(m), at] + rb[m, i, 3, :, here].astype(F32) + rb[m, i, 4, :, here].astype(F32)
        return accD[hidden(m), at] + rb[m, i, 2, :, here].astype(F32) + rb[m, i, 5, :, here].astype(F32)

    def y_sum(m, i):
        return remote(ys.at[m, i], yr.at[m, i], sy.at[m, i], ry.at[m, i], to_slice)

    def c_sum(m, i):
        return remote(cs.at[m, i], cb.at[m, i], sc.at[m, i], rc.at[m, i], to_core)

    def y_out(m, i):
        for n in (2, 3, 4, 5):
            x_sum(m, i, n).wait_recv()

        @pl.when(jnp.logical_not(home))
        def _():
            for a in (0, 1):
                ys[m, i, a] = part(m, i, a, 0, H4).astype(BF16)
            y_sum(m, i).start()

    def y_in(m, i):
        @pl.when(jnp.logical_not(home))
        def _():
            c_sum(m, i).wait_recv()

        @pl.when(home)
        def _():
            y_sum(m, i).wait_recv()
            theirs = pl.multiple_of((1 - core) * 128, 128)
            mine = pl.multiple_of(core * 128, 128)
            for a in (0, 1):
                cs[m, i, a] = (
                    part(m, i, a, theirs, 128) + yr[m, i, a, :, pl.ds(theirs, 128)].astype(F32)
                ).astype(BF16)
            c_sum(m, i).start()
            for a in (0, 1):
                cb[m, i, a] = (
                    part(m, i, a, mine, 128) + yr[m, i, a, :, pl.ds(mine, 128)].astype(F32)
                ).astype(BF16)

    def z_sum(m):
        return remote(cb.at[m, 0], zr.at[m], sz.at[m], rz.at[m], to_zhi)

    def outer_step(m):
        scale = inner_rate / 16
        z_sum(m).wait_recv()
        mean = (cb[m, 1, 0].astype(F32) + zr[m, 0].astype(F32)).T * scale
        moment = momentum_factor * muv[:, hidden(m)] + mean
        o_mu[:, hidden(m)] = moment
        W[rep, m, 0] = (
            us[:, hidden(m)].astype(F32) - outer_rate * (mean + momentum_factor * moment)
        ).astype(BF16)
        mean = (cb[m, 1, 1].astype(F32) + zr[m, 1].astype(F32)) * scale
        moment = momentum_factor * mdv[hidden(m), :] + mean
        o_md[hidden(m), :] = moment
        W[rep, m, 1] = (
            ds[hidden(m), :].astype(F32) - outer_rate * (mean + momentum_factor * moment)
        ).astype(BF16)
        go(a_z(m))
        x_out(0, m)

    back_by = {0: 0, 1: 1, 2: 2, 3: -1}

    def share(q, j, cc):
        return (((x - back_by[j] + 4) % 4) * 2 + (zhi + q) % 2) * 2 + cc

    def a_z(m):
        block = W.at[rep, m]
        return remote(block, block, sA.at[1, 0, m, 0], rA.at[1, 0, m, 0], to_zhi)

    def z_in(m):
        block = W.at[share(1, 0, core), m]
        return remote(block, block, sA.at[1, 0, m, 0], rA.at[1, 0, m, 0], to_zhi)

    def a_x(a, m, q, j, dst_j, to):
        block = W.at[share(q, j, core), m, a]
        return remote(block, block, sA.at[q, dst_j, m, a], rA.at[q, dst_j, m, a], to)

    def x_in(a, m, q, j):
        block = W.at[share(q, j, core), m, a]
        return remote(block, block, sA.at[q, j, m, a], rA.at[q, j, m, a], to_right)

    def a_c(m, q, j):
        block = W.at[share(q, j, core), m]
        return remote(block, block, sC.at[q, j, m], rC.at[q, j, m], to_core)

    def c_in(m, q, j):
        block = W.at[share(q, j, 1 - core), m]
        return remote(block, block, sC.at[q, j, m], rC.at[q, j, m], to_core)

    def place(m, q, j, cc):
        r = share(q, j, cc)
        at = pl.ds(pl.multiple_of(r * 128, 128), 128)
        o_up[at, hidden(m)] = W[r, m, 0]
        o_dn[hidden(m), at] = W[r, m, 1]

    def x_out(q, m):
        if q == 1:
            z_in(m).wait_recv()
        go(a_x(0, m, q, 0, 1, to_right))
        go(a_x(1, m, q, 0, 3, to_left))
        go(a_x(1, m, q, 0, 1, to_right))
        go(a_x(0, m, q, 0, 3, to_left))
        go(a_c(m, q, 0))

    def x_pass(q, m):
        x_in(0, m, q, 1).wait_recv()
        go(a_x(0, m, q, 1, 2, to_right))
        x_in(1, m, q, 3).wait_recv()
        go(a_x(1, m, q, 3, 2, to_left))
        x_in(1, m, q, 1).wait_recv()
        go(a_c(m, q, 1))
        x_in(0, m, q, 3).wait_recv()
        go(a_c(m, q, 3))
        place(m, q, 0, core)
        place(m, q, 1, core)
        place(m, q, 3, core)
        for a in (0, 1):
            x_in(a, m, q, 2).wait_recv()
        go(a_c(m, q, 2))
        place(m, q, 2, core)

    def from_other(q, m):
        for j in (0, 1, 3, 2):
            c_in(m, q, j).wait_recv()
            place(m, q, j, 1 - core)

    def settle(copies):
        for c in copies:
            c.wait_send()

    x_first(0, 0)
    x_relay(0, 0)
    x_first(1, 0)
    y_out(0, 0)
    x_relay(1, 0)
    x_first(0, 1)
    y_in(0, 0)
    go(z_sum(0))
    y_out(1, 0)
    x_relay(0, 1)
    x_first(1, 1)
    y_in(1, 0)
    go(z_sum(1))
    y_out(0, 1)
    x_relay(1, 1)
    y_in(0, 1)
    y_out(1, 1)
    for c in loads[2:]:
        c.wait()
    early = list(sent)
    sent.clear()
    outer_step(0)
    y_in(1, 1)
    x_pass(0, 0)

    outer_step(1)
    settle(early)

    @pl.when(home)
    def _():
        for c in w_send:
            c.wait_send()
        for m in (0, 1):
            for i in (0, 1):
                c_sum(m, i).wait_send()

    @pl.when(jnp.logical_not(home))
    def _():
        for m in (0, 1):
            for i in (0, 1):
                y_sum(m, i).wait_send()

    from_other(0, 0)
    x_out(1, 0)
    x_pass(0, 1)
    x_pass(1, 0)
    from_other(0, 1)
    x_out(1, 1)
    from_other(1, 0)
    x_pass(1, 1)
    from_other(1, 1)
    settle(sent)


def local(tokens_in, cotangent, up_weight, down_weight, up_moment, down_moment):
    dma = pltpu.SemaphoreType.DMA
    vmem = pltpu.VMEM
    return pl.pallas_call(
        outer_round,
        out_shape=(
            jax.ShapeDtypeStruct(up_weight.shape, BF16),
            jax.ShapeDtypeStruct(down_weight.shape, BF16),
            jax.ShapeDtypeStruct(up_moment.shape, F32),
            jax.ShapeDtypeStruct(down_moment.shape, F32),
        ),
        in_specs=[pl.BlockSpec(memory_space=pltpu.HBM)] * 6,
        out_specs=[pl.BlockSpec(memory_space=pltpu.VMEM)] * 4,
        scratch_shapes=[
            vmem((8 * SLAB, D), BF16), vmem((8 * SLAB, D), BF16),
            vmem((D, FL), BF16), vmem((FL, D), BF16),
            vmem((FL, D), F32), vmem((FL, D), F32),
            vmem((FL, SLAB), BF16), vmem((FL, SLAB), BF16),
            vmem((2, 2, 6, FL // 2, Q4 // 2), BF16), vmem((2, 2, 6, FL // 2, Q4 // 2), BF16),
            vmem((2, 2, 2, FL // 2, Q4 // 2), BF16), vmem((2, 2, 2, FL // 2, Q4 // 2), BF16),
            vmem((2, 2, 2, FL // 2, 128), BF16), vmem((2, 2, 2, FL // 2, 128), BF16),
            vmem((2, 2, FL // 2, 128), BF16),
            vmem((128, FL), BF16), vmem((FL, 128), BF16),
            vmem((128, FL), F32), vmem((FL, 128), F32),
            vmem((16, 2, 2, FL // 2, 128), BF16),
            dma((6,)),
            dma((8,)), dma((8,)), dma((8, 2)), dma((8, 2)), dma((8,)), dma((8,)), dma((1,)), dma((1,)),
            dma((8, 2)), dma((8, 2)), dma((8, 2)), dma((8, 2)), dma((4,)), dma((2,)),
            dma((2, 2, 6)), dma((2, 2, 6)), dma((2, 2)), dma((2, 2)), dma((2, 2)), dma((2, 2)), dma((2,)), dma((2,)),
            dma((2, 4, 2, 2)), dma((2, 4, 2, 2)), dma((2, 4, 2)), dma((2, 4, 2)),
        ],
        compiler_params=pltpu.CompilerParams(
            collective_id=0, has_side_effects=True, vmem_limit_bytes=60 << 20
        ),
        name="outer_round",
    )(tokens_in[0], cotangent[0], up_weight, down_weight, up_moment, down_moment)


def solution(mesh):
    return jax.shard_map(
        local,
        mesh=mesh,
        in_specs=(
            P("rep", "fsdp", None),
            P("rep", "fsdp", None),
            P(None, "fsdp"),
            P("fsdp", None),
            P("rep", "fsdp"),
            P("fsdp", "rep"),
        ),
        out_specs=(P(None, "fsdp"), P("fsdp", None), P("rep", "fsdp"), P("fsdp", "rep")),
        check_vma=False,
    )
```

```python
import functools

import jax
import jax.numpy as jnp
from jax import lax
from jax.experimental import pallas as pl
from jax.experimental.pallas import tpu as pltpu
from jax.sharding import PartitionSpec as P

inner_rate = 0.3
outer_rate = 0.7
momentum_factor = 0.9

MESH = pl.DeviceIdType.MESH
F32 = jnp.float32
BF16 = jnp.bfloat16

ROWS = 48
SLAB = 4 * ROWS
D = 2048
FL = 256
Q4 = D // 4


def device(x, zhi, core, zlo, y):
    return {"rep": (x * 2 + zhi) * 2 + core, "fsdp": zlo * 4 + y}


def outer_round(
    tok, cot, up, down, mu, md,
    o_up, o_dn, o_mu, o_md,
    X, G, Wu, Wd, accU, accD, dT, aT, sb, rb, ys, yr, cs, cr, cb, zr, us, ds, muv, mdv, W,
    ld, sxz, rxz, sgz, rgz, sxy, rxy, sgy, rgy, sxc, rxc, sgc, rgc, sw, rw,
    sx, rx, sy, ry, sc, rc, sz, rz, sA, rA, sC, rC, notes,
):
    rep = lax.axis_index("rep")
    fs = lax.axis_index("fsdp")
    x, zhi, core = rep // 4, (rep // 2) % 2, rep % 2
    zlo, y = fs // 4, fs % 4
    z = zhi * 8 + zlo
    sgn = 1 - 2 * core

    def at_z(zz):
        zz = (zz + 32) % 16
        return device(x, zz // 8, core, zz % 8, y)

    def at_x(xx):
        return device((xx + 8) % 4, zhi, core, zlo, y)

    to_long = at_z(z + sgn)
    to_short = at_z(z - sgn)
    to_pair = device(x, zhi, core, zlo, y + 1 - 2 * (y % 2))
    to_slice = device(x, zhi, core, zlo, 3 - y)
    to_core = device(x, zhi, 1 - core, zlo, y)
    to_cross = device(x, zhi, 1 - core, zlo, 3 - y)
    to_across = at_x(x + 2)
    to_right = at_x(x + 1)
    to_left = at_x(x - 1)
    to_zhi = device(x, 1 - zhi, core, zlo, y)
    home = (y % 2) == core

    def local(src, dst, sem):
        return pltpu.make_async_copy(src, dst, sem)

    def remote(src, dst, ssem, rsem, to):
        return pltpu.make_async_remote_copy(
            src_ref=src, dst_ref=dst, send_sem=ssem, recv_sem=rsem,
            device_id=to, device_id_type=MESH,
        )

    def slot(buf, zi, yi, ci):
        return buf.at[pl.ds(zi * SLAB + (yi * 2 + ci) * ROWS, ROWS), :]

    share_row = pl.multiple_of(rep * 128, 128)
    loads = [
        local(tok, slot(X, 0, 0, 0), ld.at[0]),
        local(cot, slot(G, 0, 0, 0), ld.at[1]),
        local(up.at[pl.ds(share_row, 128), :], us, ld.at[2]),
        local(down.at[:, pl.ds(share_row, 128)], ds, ld.at[3]),
        local(mu, muv, ld.at[4]),
        local(md, mdv, ld.at[5]),
    ]
    for c in loads:
        c.start()

    barrier = pltpu.get_barrier_semaphore()
    everyone = (
        to_long, to_short, to_pair, to_slice, to_core, to_cross, to_right, to_left, to_across,
    )
    for other in everyone:
        pl.semaphore_signal(barrier, inc=1, device_id=other, device_id_type=MESH)
    loads[0].wait()
    loads[1].wait()
    pl.semaphore_wait(barrier, len(everyone))

    def pass_note(k):
        if k > 0:
            pl.semaphore_wait(notes.at[k - 1], 1)
        if k < 7:
            pl.semaphore_signal(notes.at[k], inc=1, device_id=to_long, device_id_type=MESH)

    pass_note(0)

    sent = []

    def go(copy):
        copy.start()
        sent.append(copy)

    def x_z(src_zi, dst_zi, to):
        return remote(slot(X, src_zi, 0, 0), slot(X, dst_zi, 0, 0), sxz.at[dst_zi], rxz.at[dst_zi], to)

    def g_z(src_zi, dst_zi, yi, to):
        return remote(
            slot(G, src_zi, yi, 0), slot(G, dst_zi, yi, 0), sgz.at[dst_zi, yi], rgz.at[dst_zi, yi], to
        )

    def x_y(zi):
        return remote(slot(X, zi, 0, 0), slot(X, zi, 1, 0), sxy.at[zi], rxy.at[zi], to_pair)

    def g_y():
        return remote(slot(G, 0, 0, 0), slot(G, 0, 1, 0), sgy.at[0], rgy.at[0], to_pair)

    def x_c(zi, yi):
        return remote(slot(X, zi, yi, 0), slot(X, zi, yi, 1), sxc.at[zi, yi], rxc.at[zi, yi], to_core)

    def g_c(zi, yi):
        return remote(slot(G, zi, yi, 0), slot(G, zi, yi, 1), sgc.at[zi, yi], rgc.at[zi, yi], to_core)

    go(g_y())
    go(x_z(0, 1, to_long))
    go(x_z(0, 2, to_short))
    go(g_z(0, 1, 0, to_long))
    go(g_z(0, 2, 0, to_short))
    go(x_y(0))
    go(x_c(0, 0))
    go(g_c(0, 0))

    w_send = [
        remote(up, Wu, sw.at[0], rw.at[0], to_slice),
        remote(down, Wd, sw.at[1], rw.at[1], to_slice),
    ]
    w_local = [local(up, Wu, sw.at[2]), local(down, Wd, sw.at[3])]

    @pl.when(home)
    def _():
        for c in w_send + w_local:
            c.start()

    pass_note(1)
    g_y().wait_recv()
    go(g_z(0, 1, 1, to_long))
    go(g_z(0, 2, 1, to_short))
    go(g_c(0, 1))
    x_y(0).wait_recv()
    go(x_c(0, 1))
    pass_note(2)

    def arrived_x(zi, onward, to):
        x_z(0, zi, to_long).wait_recv()
        if onward:
            go(x_z(zi, zi + 2, to))
        go(x_y(zi))
        go(x_c(zi, 0))

    def arrived_g(zi, yi, onward, to):
        g_z(0, zi, yi, to_long).wait_recv()
        if onward:
            go(g_z(zi, zi + 2, yi, to))
        go(g_c(zi, yi))

    def arrived_pair(zi):
        x_y(zi).wait_recv()
        go(x_c(zi, 1))

    def from_core(zi):
        for yi in (0, 1):
            x_c(zi, yi).wait_recv()
            g_c(zi, yi).wait_recv()

    def middle(zi):
        rows = pl.ds(zi * SLAB, SLAB)
        pre = jnp.dot(X[rows, :], Wu[...], preferred_element_type=F32)
        back = lax.dot_general(G[rows, :], Wd[...], (((1,), (1,)), ((), ())), preferred_element_type=F32)
        s = jax.nn.sigmoid(pre)
        act = pre * s
        dpre = back * s * (1.0 + pre * (1.0 - s))
        dT[...] = dpre.astype(BF16).T
        aT[...] = act.astype(BF16).T

    def grads(zi):
        rows = pl.ds(zi * SLAB, SLAB)

        @pl.loop(0, D // 256)
        def _(j):
            cols = pl.ds(pl.multiple_of(j * 256, 256), 256)
            du = jnp.dot(dT[...], X[rows, cols], preferred_element_type=F32)
            dd = jnp.dot(aT[...], G[rows, cols], preferred_element_type=F32)
            accU[:, cols] = du if zi == 0 else accU[:, cols] + du
            accD[:, cols] = dd if zi == 0 else accD[:, cols] + dd

    def unit(zi):
        from_core(zi)
        middle(zi)
        grads(zi)

    for k in (1, 2, 3):
        long, short = 2 * k - 1, 2 * k
        arrived_x(long, True, to_long)
        arrived_x(short, k < 3, to_short)
        if k < 3:
            pass_note(2 * k + 1)
        if k == 3:
            unit(1)
        arrived_g(long, 0, True, to_long)
        arrived_g(short, 0, k < 3, to_short)
        if k == 3:
            unit(2)
        arrived_pair(long)
        arrived_pair(short)
        if k == 3:
            unit(3)
        arrived_g(long, 1, True, to_long)
        arrived_g(short, 1, k < 3, to_short)
        if k < 3:
            pass_note(2 * k + 2)
        else:
            pass_note(7)
        if k == 2:

            @pl.when(home)
            def _():
                for c in w_local:
                    c.wait()

            @pl.when(jnp.logical_not(home))
            def _():
                for c in w_send:
                    c.wait_recv()

            unit(0)
        if k == 3:
            unit(4)

    arrived_x(7, False, to_long)
    unit(5)
    arrived_g(7, 0, False, to_long)
    unit(6)
    arrived_pair(7)
    arrived_g(7, 1, False, to_long)
    from_core(7)
    middle(7)

    last = pl.ds(7 * SLAB, SLAB)
    H4 = Q4 // 2
    HR = FL // 2
    half = (1 - zhi, zhi)

    def hidden(m):
        return pl.ds(m * HR, HR)

    def cols(step, i):
        return pl.ds(pl.multiple_of(((x + step) % 4) * Q4 + half[i] * H4, H4), H4)

    def total_up(m, at):
        return accU[hidden(m), at] + jnp.dot(dT[hidden(m), :], X[last, at], preferred_element_type=F32)

    def total_dn(m, at):
        return accD[hidden(m), at] + jnp.dot(aT[hidden(m), :], G[last, at], preferred_element_type=F32)

    def x_sum(m, i, n):
        return remote(
            sb.at[m, i, n], rb.at[m, i, n], sx.at[m, i, n], rx.at[m, i, n],
            to_right if n % 2 == 0 else to_left,
        )

    def x_first(m, i):
        sb[m, i, 0] = total_up(m, cols(2, i)).astype(BF16)
        go(x_sum(m, i, 0))
        sb[m, i, 1] = total_dn(m, cols(2, i)).astype(BF16)
        go(x_sum(m, i, 1))
        sb[m, i, 2] = total_dn(m, cols(1, i)).astype(BF16)
        go(x_sum(m, i, 2))
        sb[m, i, 3] = total_up(m, cols(3, i)).astype(BF16)
        go(x_sum(m, i, 3))
        for step in (1, 0):
            accU[hidden(m), cols(step, i)] = total_up(m, cols(step, i))
        for step in (3, 0):
            accD[hidden(m), cols(step, i)] = total_dn(m, cols(step, i))

    def x_relay(m, i):
        x_sum(m, i, 0).wait_recv()
        sb[m, i, 4] = (accU[hidden(m), cols(1, i)] + rb[m, i, 0].astype(F32)).astype(BF16)
        go(x_sum(m, i, 4))
        x_sum(m, i, 1).wait_recv()
        sb[m, i, 5] = (accD[hidden(m), cols(3, i)] + rb[m, i, 1].astype(F32)).astype(BF16)
        go(x_sum(m, i, 5))

    def part(m, i, a, off, width):
        at = pl.ds(pl.multiple_of(x * Q4 + half[i] * H4 + off, 128), width)
        here = pl.ds(pl.multiple_of(off, 128), width)
        if a == 0:
            return accU[hidden(m), at] + rb[m, i, 3, :, here].astype(F32) + rb[m, i, 4, :, here].astype(F32)
        return accD[hidden(m), at] + rb[m, i, 2, :, here].astype(F32) + rb[m, i, 5, :, here].astype(F32)

    def y_home(m, i):
        return remote(ys.at[m, i, 0], yr.at[m, i], sy.at[m, i, 0], ry.at[m, i], to_slice)

    def y_cross(m, i):
        return remote(ys.at[m, i, 1], yr.at[m, i], sy.at[m, i, 1], ry.at[m, i], to_cross)

    def c_sum(m, i):
        return remote(cs.at[m, i], cr.at[m, i], sc.at[m, i], rc.at[m, i], to_core)

    mine = pl.multiple_of(core * 128, 128)
    theirs = pl.multiple_of((1 - core) * 128, 128)

    def y_out(m, i):
        for n in (2, 3, 4, 5):
            x_sum(m, i, n).wait_recv()

        @pl.when(jnp.logical_not(home))
        def _():
            for a in (0, 1):
                ys[m, i, 0, a] = part(m, i, a, mine, 128).astype(BF16)
            y_home(m, i).start()
            for a in (0, 1):
                ys[m, i, 1, a] = part(m, i, a, theirs, 128).astype(BF16)
            y_cross(m, i).start()

        @pl.when(home)
        def _():
            for a in (0, 1):
                cs[m, i, a] = part(m, i, a, theirs, 128).astype(BF16)
            c_sum(m, i).start()

    def y_in(m, i):
        @pl.when(jnp.logical_not(home))
        def _():
            c_sum(m, i).wait_recv()
            y_cross(m, i).wait_recv()
            for a in (0, 1):
                cb[m, i, a] = (cr[m, i, a].astype(F32) + yr[m, i, a].astype(F32)).astype(BF16)

        @pl.when(home)
        def _():
            y_home(m, i).wait_recv()
            for a in (0, 1):
                cb[m, i, a] = (part(m, i, a, mine, 128) + yr[m, i, a].astype(F32)).astype(BF16)

    def z_sum(m):
        return remote(cb.at[m, 0], zr.at[m], sz.at[m], rz.at[m], to_zhi)

    def outer_step(m):
        scale = inner_rate / 16
        z_sum(m).wait_recv()
        mean = (cb[m, 1, 0].astype(F32) + zr[m, 0].astype(F32)).T * scale
        moment = momentum_factor * muv[:, hidden(m)] + mean
        o_mu[:, hidden(m)] = moment
        W[rep, m, 0] = (
            us[:, hidden(m)].astype(F32) - outer_rate * (mean + momentum_factor * moment)
        ).astype(BF16)
        mean = (cb[m, 1, 1].astype(F32) + zr[m, 1].astype(F32)) * scale
        moment = momentum_factor * mdv[hidden(m), :] + mean
        o_md[hidden(m), :] = moment
        W[rep, m, 1] = (
            ds[hidden(m), :].astype(F32) - outer_rate * (mean + momentum_factor * moment)
        ).astype(BF16)
        go(a_z(m))
        x_out(0, m)

    back_by = {0: 0, 1: 1, 2: 2, 3: -1}

    def share(q, j, cc):
        return (((x - back_by[j] + 4) % 4) * 2 + (zhi + q) % 2) * 2 + cc

    def a_z(m):
        block = W.at[rep, m]
        return remote(block, block, sA.at[1, 0, m], rA.at[1, 0, m], to_zhi)

    def z_in(m):
        block = W.at[share(1, 0, core), m]
        return remote(block, block, sA.at[1, 0, m], rA.at[1, 0, m], to_zhi)

    def a_x(m, q, dst_j, to):
        block = W.at[share(q, 0, core), m]
        return remote(block, block, sA.at[q, dst_j, m], rA.at[q, dst_j, m], to)

    def x_in(m, q, j):
        block = W.at[share(q, j, core), m]
        return remote(block, block, sA.at[q, j, m], rA.at[q, j, m], to_right)

    def a_c(m, q, j):
        block = W.at[share(q, j, core), m]
        return remote(block, block, sC.at[q, j, m], rC.at[q, j, m], to_core)

    def c_in(m, q, j):
        block = W.at[share(q, j, 1 - core), m]
        return remote(block, block, sC.at[q, j, m], rC.at[q, j, m], to_core)

    def place(m, q, j, cc):
        r = share(q, j, cc)
        at = pl.ds(pl.multiple_of(r * 128, 128), 128)
        o_up[at, hidden(m)] = W[r, m, 0]
        o_dn[hidden(m), at] = W[r, m, 1]

    def x_out(q, m):
        if q == 1:
            z_in(m).wait_recv()
        go(a_x(m, q, 2, to_across))
        go(a_x(m, q, 1, to_right))
        go(a_x(m, q, 3, to_left))
        go(a_c(m, q, 0))

    def x_pass(q, m):
        place(m, q, 0, core)
        for j in (1, 3, 2):
            x_in(m, q, j).wait_recv()
            go(a_c(m, q, j))
            place(m, q, j, core)

    def from_other(q, m):
        for j in (0, 1, 3, 2):
            c_in(m, q, j).wait_recv()
            place(m, q, j, 1 - core)

    def settle(copies):
        for c in copies:
            c.wait_send()

    x_first(0, 0)
    x_relay(0, 0)
    x_first(1, 0)
    y_out(0, 0)
    x_relay(1, 0)
    x_first(0, 1)
    y_in(0, 0)
    go(z_sum(0))
    y_out(1, 0)
    x_relay(0, 1)
    x_first(1, 1)
    y_in(1, 0)
    go(z_sum(1))
    y_out(0, 1)
    x_relay(1, 1)
    y_in(0, 1)
    y_out(1, 1)
    for c in loads[2:]:
        c.wait()
    early = list(sent)
    sent.clear()
    outer_step(0)
    y_in(1, 1)
    x_pass(0, 0)

    outer_step(1)
    settle(early)

    @pl.when(home)
    def _():
        for c in w_send:
            c.wait_send()
        for m in (0, 1):
            for i in (0, 1):
                c_sum(m, i).wait_send()

    @pl.when(jnp.logical_not(home))
    def _():
        for m in (0, 1):
            for i in (0, 1):
                y_home(m, i).wait_send()
                y_cross(m, i).wait_send()

    from_other(0, 0)
    x_out(1, 0)
    x_pass(0, 1)
    x_pass(1, 0)
    from_other(0, 1)
    x_out(1, 1)
    from_other(1, 0)
    x_pass(1, 1)
    from_other(1, 1)
    settle(sent)


def local(tokens_in, cotangent, up_weight, down_weight, up_moment, down_moment):
    dma = pltpu.SemaphoreType.DMA
    vmem = pltpu.VMEM
    return pl.pallas_call(
        outer_round,
        out_shape=(
            jax.ShapeDtypeStruct(up_weight.shape, BF16),
            jax.ShapeDtypeStruct(down_weight.shape, BF16),
            jax.ShapeDtypeStruct(up_moment.shape, F32),
            jax.ShapeDtypeStruct(down_moment.shape, F32),
        ),
        in_specs=[pl.BlockSpec(memory_space=pltpu.HBM)] * 6,
        out_specs=[pl.BlockSpec(memory_space=pltpu.VMEM)] * 4,
        scratch_shapes=[
            vmem((8 * SLAB, D), BF16), vmem((8 * SLAB, D), BF16),
            vmem((D, FL), BF16), vmem((FL, D), BF16),
            vmem((FL, D), F32), vmem((FL, D), F32),
            vmem((FL, SLAB), BF16), vmem((FL, SLAB), BF16),
            vmem((2, 2, 6, FL // 2, Q4 // 2), BF16), vmem((2, 2, 6, FL // 2, Q4 // 2), BF16),
            vmem((2, 2, 2, 2, FL // 2, 128), BF16), vmem((2, 2, 2, FL // 2, 128), BF16),
            vmem((2, 2, 2, FL // 2, 128), BF16), vmem((2, 2, 2, FL // 2, 128), BF16),
            vmem((2, 2, 2, FL // 2, 128), BF16),
            vmem((2, 2, FL // 2, 128), BF16),
            vmem((128, FL), BF16), vmem((FL, 128), BF16),
            vmem((128, FL), F32), vmem((FL, 128), F32),
            vmem((16, 2, 2, FL // 2, 128), BF16),
            dma((6,)),
            dma((8,)), dma((8,)), dma((8, 2)), dma((8, 2)), dma((8,)), dma((8,)), dma((1,)), dma((1,)),
            dma((8, 2)), dma((8, 2)), dma((8, 2)), dma((8, 2)), dma((4,)), dma((2,)),
            dma((2, 2, 6)), dma((2, 2, 6)), dma((2, 2, 2)), dma((2, 2)), dma((2, 2)), dma((2, 2)), dma((2,)), dma((2,)),
            dma((2, 4, 2)), dma((2, 4, 2)), dma((2, 4, 2)), dma((2, 4, 2)),
            pltpu.SemaphoreType.REGULAR((7,)),
        ],
        compiler_params=pltpu.CompilerParams(
            collective_id=0, has_side_effects=True, vmem_limit_bytes=60 << 20
        ),
        name="outer_round",
    )(tokens_in[0], cotangent[0], up_weight, down_weight, up_moment, down_moment)


def solution(mesh):
    return jax.shard_map(
        local,
        mesh=mesh,
        in_specs=(
            P("rep", "fsdp", None),
            P("rep", "fsdp", None),
            P(None, "fsdp"),
            P("fsdp", None),
            P("rep", "fsdp"),
            P("fsdp", "rep"),
        ),
        out_specs=(P(None, "fsdp"), P("fsdp", None), P("rep", "fsdp"), P("fsdp", "rep")),
        check_vma=False,
    )
```

```python
import functools

import jax
import jax.numpy as jnp
from jax import lax
from jax.experimental import pallas as pl
from jax.experimental.pallas import tpu as pltpu
from jax.sharding import PartitionSpec as P

inner_rate = 0.3
outer_rate = 0.7
momentum_factor = 0.9

MESH = pl.DeviceIdType.MESH
F32 = jnp.float32
BF16 = jnp.bfloat16

ROWS = 48
SLAB = 4 * ROWS
D = 2048
FL = 256
Q4 = D // 4


def device(x, zhi, core, zlo, y):
    return {"rep": (x * 2 + zhi) * 2 + core, "fsdp": zlo * 4 + y}


def outer_round(
    tok, cot, up, down, mu, md,
    o_up, o_dn, o_mu, o_md,
    X, G, Wu, Wd, accU, accD, dT, aT, sb, rb, ys, yr, cs, cr, cb, zr, us, ds, muv, mdv, W,
    ld, sxz, rxz, sgz, rgz, sxy, rxy, sgy, rgy, sxc, rxc, sgc, rgc, sw, rw,
    sx, rx, sy, ry, sc, rc, sz, rz, sA, rA, sC, rC, sw2, rw2, notes,
):
    rep = lax.axis_index("rep")
    fs = lax.axis_index("fsdp")
    x, zhi, core = rep // 4, (rep // 2) % 2, rep % 2
    zlo, y = fs // 4, fs % 4
    z = zhi * 8 + zlo
    sgn = 1 - 2 * core

    def at_z(zz):
        zz = (zz + 32) % 16
        return device(x, zz // 8, core, zz % 8, y)

    def at_x(xx):
        return device((xx + 8) % 4, zhi, core, zlo, y)

    to_long = at_z(z + sgn)
    to_short = at_z(z - sgn)
    to_pair = device(x, zhi, core, zlo, y + 1 - 2 * (y % 2))
    to_slice = device(x, zhi, core, zlo, 3 - y)
    to_core = device(x, zhi, 1 - core, zlo, y)
    to_cross = device(x, zhi, 1 - core, zlo, 3 - y)
    to_across = at_x(x + 2)
    to_right = at_x(x + 1)
    to_left = at_x(x - 1)
    to_zhi = device(x, 1 - zhi, core, zlo, y)
    home = (y % 2) == core

    def local(src, dst, sem):
        return pltpu.make_async_copy(src, dst, sem)

    def remote(src, dst, ssem, rsem, to):
        return pltpu.make_async_remote_copy(
            src_ref=src, dst_ref=dst, send_sem=ssem, recv_sem=rsem,
            device_id=to, device_id_type=MESH,
        )

    def slot(buf, zi, yi, ci):
        return buf.at[pl.ds(zi * SLAB + (yi * 2 + ci) * ROWS, ROWS), :]

    share_row = pl.multiple_of(rep * 128, 128)
    loads = [
        local(tok, slot(X, 0, 0, 0), ld.at[0]),
        local(cot, slot(G, 0, 0, 0), ld.at[1]),
        local(up.at[pl.ds(share_row, 128), :], us, ld.at[2]),
        local(down.at[:, pl.ds(share_row, 128)], ds, ld.at[3]),
        local(mu, muv, ld.at[4]),
        local(md, mdv, ld.at[5]),
    ]
    for c in loads:
        c.start()

    barrier = pltpu.get_barrier_semaphore()
    everyone = (
        to_long, to_short, to_pair, to_slice, to_core, to_cross, to_right, to_left, to_across,
    )
    for other in everyone:
        pl.semaphore_signal(barrier, inc=1, device_id=other, device_id_type=MESH)
    loads[0].wait()
    loads[1].wait()
    pl.semaphore_wait(barrier, len(everyone))

    def pass_note(k):
        if k > 0:
            pl.semaphore_wait(notes.at[k - 1], 1)
        if k < 7:
            pl.semaphore_signal(notes.at[k], inc=1, device_id=to_long, device_id_type=MESH)

    pass_note(0)

    sent = []

    def go(copy):
        copy.start()
        sent.append(copy)

    def x_z(src_zi, dst_zi, to):
        return remote(slot(X, src_zi, 0, 0), slot(X, dst_zi, 0, 0), sxz.at[dst_zi], rxz.at[dst_zi], to)

    def g_z(src_zi, dst_zi, yi, to):
        return remote(
            slot(G, src_zi, yi, 0), slot(G, dst_zi, yi, 0), sgz.at[dst_zi, yi], rgz.at[dst_zi, yi], to
        )

    def x_y(zi):
        return remote(slot(X, zi, 0, 0), slot(X, zi, 1, 0), sxy.at[zi], rxy.at[zi], to_pair)

    def g_y(zi):
        return remote(slot(G, zi, 0, 0), slot(G, zi, 1, 0), sgy.at[zi], rgy.at[zi], to_pair)

    def x_c(zi, yi):
        return remote(slot(X, zi, yi, 0), slot(X, zi, yi, 1), sxc.at[zi, yi], rxc.at[zi, yi], to_core)

    def g_c(zi, yi):
        return remote(slot(G, zi, yi, 0), slot(G, zi, yi, 1), sgc.at[zi, yi], rgc.at[zi, yi], to_core)

    go(g_y(0))
    go(x_z(0, 1, to_long))
    go(x_z(0, 2, to_short))
    go(g_z(0, 1, 0, to_long))
    go(g_z(0, 2, 0, to_short))
    go(x_y(0))
    go(x_c(0, 0))
    go(g_c(0, 0))

    w_send = [
        remote(up, Wu, sw.at[0], rw.at[0], to_slice),
        remote(down, Wd, sw.at[1], rw.at[1], to_slice),
    ]
    w_local = [local(up, Wu, sw.at[2]), local(down, Wd, sw.at[3])]

    @pl.when(home)
    def _():
        for c in w_send + w_local:
            c.start()

    pass_note(1)
    g_y(0).wait_recv()
    go(g_z(0, 2, 1, to_short))
    go(g_c(0, 1))
    x_y(0).wait_recv()
    go(x_c(0, 1))
    pass_note(2)

    def arrived_x(zi, onward, to):
        x_z(0, zi, to_long).wait_recv()
        if onward:
            go(x_z(zi, zi + 2, to))
        if zi != 2:
            go(x_y(zi))
        go(x_c(zi, 0))

    def arrived_g(zi, yi, onward, to):
        g_z(0, zi, yi, to_long).wait_recv()
        if onward:
            go(g_z(zi, zi + 2, yi, to))
        if zi == 1:
            go(g_y(1))
            go(x_y(2))
        go(g_c(zi, yi))

    def arrived_pair(zi):
        x_y(zi).wait_recv()
        go(x_c(zi, 1))

    def from_core(zi):
        for yi in (0, 1):
            x_c(zi, yi).wait_recv()
            g_c(zi, yi).wait_recv()

    def middle(zi):
        rows = pl.ds(zi * SLAB, SLAB)
        pre = jnp.dot(X[rows, :], Wu[...], preferred_element_type=F32)
        back = lax.dot_general(G[rows, :], Wd[...], (((1,), (1,)), ((), ())), preferred_element_type=F32)
        s = jax.nn.sigmoid(pre)
        act = pre * s
        dpre = back * s * (1.0 + pre * (1.0 - s))
        dT[...] = dpre.astype(BF16).T
        aT[...] = act.astype(BF16).T

    def grads(zi):
        rows = pl.ds(zi * SLAB, SLAB)

        @pl.loop(0, D // 256)
        def _(j):
            cols = pl.ds(pl.multiple_of(j * 256, 256), 256)
            du = jnp.dot(dT[...], X[rows, cols], preferred_element_type=F32)
            dd = jnp.dot(aT[...], G[rows, cols], preferred_element_type=F32)
            accU[:, cols] = du if zi == 0 else accU[:, cols] + du
            accD[:, cols] = dd if zi == 0 else accD[:, cols] + dd

    def unit(zi):
        from_core(zi)
        middle(zi)
        grads(zi)

    for k in (1, 2, 3):
        long, short = 2 * k - 1, 2 * k
        arrived_x(long, True, to_long)
        arrived_x(short, k < 3, to_short)
        if k == 2:
            g_y(1).wait_recv()
            go(g_z(1, 3, 1, to_long))
            go(g_c(1, 1))
        if k < 3:
            pass_note(2 * k + 1)
        if k == 3:
            unit(1)
        arrived_g(long, 0, True, to_long)
        arrived_g(short, 0, k < 3, to_short)
        if k == 3:
            unit(2)
        arrived_pair(long)
        arrived_pair(short)
        if k == 3:
            unit(3)
        if k > 1:
            arrived_g(long, 1, True, to_long)
        arrived_g(short, 1, k < 3, to_short)
        if k < 3:
            pass_note(2 * k + 2)
        else:
            pass_note(7)
        if k == 2:

            @pl.when(home)
            def _():
                for c in w_local:
                    c.wait()

            @pl.when(jnp.logical_not(home))
            def _():
                for c in w_send:
                    c.wait_recv()

            unit(0)
        if k == 3:
            unit(4)

    arrived_x(7, False, to_long)
    unit(5)
    arrived_g(7, 0, False, to_long)
    unit(6)
    arrived_pair(7)
    arrived_g(7, 1, False, to_long)
    from_core(7)
    middle(7)

    last = pl.ds(7 * SLAB, SLAB)
    H4 = Q4 // 2
    HR = FL // 2
    half = (1 - zhi, zhi)

    def hidden(m):
        return pl.ds(m * HR, HR)

    def cols(step, i):
        return pl.ds(pl.multiple_of(((x + step) % 4) * Q4 + half[i] * H4, H4), H4)

    def total_up(m, at):
        return accU[hidden(m), at] + jnp.dot(dT[hidden(m), :], X[last, at], preferred_element_type=F32)

    def total_dn(m, at):
        return accD[hidden(m), at] + jnp.dot(aT[hidden(m), :], G[last, at], preferred_element_type=F32)

    def x_sum(m, i, n):
        return remote(
            sb.at[m, i, n], rb.at[m, i, n], sx.at[m, i, n], rx.at[m, i, n],
            to_right if n % 2 == 0 else to_left,
        )

    def x_first(m, i):
        sb[m, i, 0] = total_up(m, cols(2, i)).astype(BF16)
        go(x_sum(m, i, 0))
        sb[m, i, 1] = total_dn(m, cols(2, i)).astype(BF16)
        go(x_sum(m, i, 1))
        sb[m, i, 2] = total_dn(m, cols(1, i)).astype(BF16)
        go(x_sum(m, i, 2))
        sb[m, i, 3] = total_up(m, cols(3, i)).astype(BF16)
        go(x_sum(m, i, 3))
        for step in (1, 0):
            accU[hidden(m), cols(step, i)] = total_up(m, cols(step, i))
        for step in (3, 0):
            accD[hidden(m), cols(step, i)] = total_dn(m, cols(step, i))

    def x_relay(m, i):
        x_sum(m, i, 0).wait_recv()
        sb[m, i, 4] = (accU[hidden(m), cols(1, i)] + rb[m, i, 0].astype(F32)).astype(BF16)
        go(x_sum(m, i, 4))
        x_sum(m, i, 1).wait_recv()
        sb[m, i, 5] = (accD[hidden(m), cols(3, i)] + rb[m, i, 1].astype(F32)).astype(BF16)
        go(x_sum(m, i, 5))

    def part(m, i, a, off, width):
        at = pl.ds(pl.multiple_of(x * Q4 + half[i] * H4 + off, 128), width)
        here = pl.ds(pl.multiple_of(off, 128), width)
        if a == 0:
            return accU[hidden(m), at] + rb[m, i, 3, :, here].astype(F32) + rb[m, i, 4, :, here].astype(F32)
        return accD[hidden(m), at] + rb[m, i, 2, :, here].astype(F32) + rb[m, i, 5, :, here].astype(F32)

    def y_home(m, i):
        return remote(ys.at[m, i, 0], yr.at[m, i], sy.at[m, i, 0], ry.at[m, i], to_slice)

    def y_cross(m, i):
        return remote(ys.at[m, i, 1], yr.at[m, i], sy.at[m, i, 1], ry.at[m, i], to_cross)

    def c_sum(m, i):
        return remote(cs.at[m, i], cr.at[m, i], sc.at[m, i], rc.at[m, i], to_core)

    mine = pl.multiple_of(core * 128, 128)
    theirs = pl.multiple_of((1 - core) * 128, 128)

    def y_out(m, i):
        for n in (2, 3, 4, 5):
            x_sum(m, i, n).wait_recv()

        @pl.when(jnp.logical_not(home))
        def _():
            for a in (0, 1):
                ys[m, i, 0, a] = part(m, i, a, mine, 128).astype(BF16)
            y_home(m, i).start()
            for a in (0, 1):
                ys[m, i, 1, a] = part(m, i, a, theirs, 128).astype(BF16)
            y_cross(m, i).start()

        @pl.when(home)
        def _():
            for a in (0, 1):
                cs[m, i, a] = part(m, i, a, theirs, 128).astype(BF16)
            c_sum(m, i).start()

    def y_in(m, i):
        @pl.when(jnp.logical_not(home))
        def _():
            c_sum(m, i).wait_recv()
            y_cross(m, i).wait_recv()
            for a in (0, 1):
                cb[m, i, a] = (cr[m, i, a].astype(F32) + yr[m, i, a].astype(F32)).astype(BF16)

        @pl.when(home)
        def _():
            y_home(m, i).wait_recv()
            for a in (0, 1):
                cb[m, i, a] = (part(m, i, a, mine, 128) + yr[m, i, a].astype(F32)).astype(BF16)

    def z_sum(m):
        return remote(cb.at[m, 0], zr.at[m], sz.at[m], rz.at[m], to_zhi)

    last_z = []

    def outer_step(m):
        scale = inner_rate / 16
        z_sum(m).wait_recv()
        mean = (cb[m, 1, 0].astype(F32) + zr[m, 0].astype(F32)).T * scale
        moment = momentum_factor * muv[:, hidden(m)] + mean
        o_mu[:, hidden(m)] = moment
        W[rep, m, 0] = (
            us[:, hidden(m)].astype(F32) - outer_rate * (mean + momentum_factor * moment)
        ).astype(BF16)
        last_z.append(a_z(0, m))
        last_z[-1].start()
        mean = (cb[m, 1, 1].astype(F32) + zr[m, 1].astype(F32)) * scale
        moment = momentum_factor * mdv[hidden(m), :] + mean
        o_md[hidden(m), :] = moment
        W[rep, m, 1] = (
            ds[hidden(m), :].astype(F32) - outer_rate * (mean + momentum_factor * moment)
        ).astype(BF16)
        last_z.append(a_z(1, m))
        last_z[-1].start()
        x_out(0, m)

    back_by = {0: 0, 1: 1, 2: 2, 3: -1}

    def share(q, j, cc):
        return (((x - back_by[j] + 4) % 4) * 2 + (zhi + q) % 2) * 2 + cc

    def a_z(a, m):
        block = W.at[rep, m, a]
        return remote(block, block, sw2.at[m, a], rw2.at[m, a], to_zhi)

    def z_in(a, m):
        block = W.at[share(1, 0, core), m, a]
        return remote(block, block, sw2.at[m, a], rw2.at[m, a], to_zhi)

    def a_x(m, q, dst_j, to):
        block = W.at[share(q, 0, core), m]
        return remote(block, block, sA.at[q, dst_j, m], rA.at[q, dst_j, m], to)

    def x_in(m, q, j):
        block = W.at[share(q, j, core), m]
        return remote(block, block, sA.at[q, j, m], rA.at[q, j, m], to_right)

    def a_c(m, q, j):
        block = W.at[share(q, j, core), m]
        return remote(block, block, sC.at[q, j, m], rC.at[q, j, m], to_core)

    def c_in(m, q, j):
        block = W.at[share(q, j, 1 - core), m]
        return remote(block, block, sC.at[q, j, m], rC.at[q, j, m], to_core)

    def place(m, q, j, cc):
        r = share(q, j, cc)
        at = pl.ds(pl.multiple_of(r * 128, 128), 128)
        o_up[at, hidden(m)] = W[r, m, 0]
        o_dn[hidden(m), at] = W[r, m, 1]

    def x_out(q, m):
        if q == 1:
            z_in(0, m).wait_recv()
            z_in(1, m).wait_recv()
        go(a_x(m, q, 2, to_across))
        go(a_x(m, q, 1, to_right))
        go(a_x(m, q, 3, to_left))
        go(a_c(m, q, 0))

    def x_pass(q, m):
        place(m, q, 0, core)
        for j in (1, 3, 2):
            x_in(m, q, j).wait_recv()
            go(a_c(m, q, j))
            place(m, q, j, core)

    def from_other(q, m):
        for j in (0, 1, 3, 2):
            c_in(m, q, j).wait_recv()
            place(m, q, j, 1 - core)

    def settle(copies):
        for c in copies:
            c.wait_send()

    x_first(0, 0)
    x_relay(0, 0)
    x_first(1, 0)
    y_out(0, 0)
    x_relay(1, 0)
    x_first(0, 1)
    y_in(0, 0)
    go(z_sum(0))
    y_out(1, 0)
    x_relay(0, 1)
    x_first(1, 1)
    y_in(1, 0)
    go(z_sum(1))
    y_out(0, 1)
    x_relay(1, 1)
    y_in(0, 1)
    y_out(1, 1)
    for c in loads[2:]:
        c.wait()
    early = list(sent)
    sent.clear()
    outer_step(0)
    y_in(1, 1)
    x_pass(0, 0)

    outer_step(1)
    settle(early)

    @pl.when(home)
    def _():
        for c in w_send:
            c.wait_send()
        for m in (0, 1):
            for i in (0, 1):
                c_sum(m, i).wait_send()

    @pl.when(jnp.logical_not(home))
    def _():
        for m in (0, 1):
            for i in (0, 1):
                y_home(m, i).wait_send()
                y_cross(m, i).wait_send()

    from_other(0, 0)
    x_out(1, 0)
    x_pass(0, 1)
    x_pass(1, 0)
    from_other(0, 1)
    settle(sent)
    sent.clear()
    x_out(1, 1)
    from_other(1, 0)
    x_pass(1, 1)
    from_other(1, 1)
    settle(sent + last_z)


def local(tokens_in, cotangent, up_weight, down_weight, up_moment, down_moment):
    dma = pltpu.SemaphoreType.DMA
    vmem = pltpu.VMEM
    return pl.pallas_call(
        outer_round,
        out_shape=(
            jax.ShapeDtypeStruct(up_weight.shape, BF16),
            jax.ShapeDtypeStruct(down_weight.shape, BF16),
            jax.ShapeDtypeStruct(up_moment.shape, F32),
            jax.ShapeDtypeStruct(down_moment.shape, F32),
        ),
        in_specs=[pl.BlockSpec(memory_space=pltpu.HBM)] * 6,
        out_specs=[pl.BlockSpec(memory_space=pltpu.VMEM)] * 4,
        scratch_shapes=[
            vmem((8 * SLAB, D), BF16), vmem((8 * SLAB, D), BF16),
            vmem((D, FL), BF16), vmem((FL, D), BF16),
            vmem((FL, D), F32), vmem((FL, D), F32),
            vmem((FL, SLAB), BF16), vmem((FL, SLAB), BF16),
            vmem((2, 2, 6, FL // 2, Q4 // 2), BF16), vmem((2, 2, 6, FL // 2, Q4 // 2), BF16),
            vmem((2, 2, 2, 2, FL // 2, 128), BF16), vmem((2, 2, 2, FL // 2, 128), BF16),
            vmem((2, 2, 2, FL // 2, 128), BF16), vmem((2, 2, 2, FL // 2, 128), BF16),
            vmem((2, 2, 2, FL // 2, 128), BF16),
            vmem((2, 2, FL // 2, 128), BF16),
            vmem((128, FL), BF16), vmem((FL, 128), BF16),
            vmem((128, FL), F32), vmem((FL, 128), F32),
            vmem((16, 2, 2, FL // 2, 128), BF16),
            dma((6,)),
            dma((8,)), dma((8,)), dma((8, 2)), dma((8, 2)), dma((8,)), dma((8,)), dma((2,)), dma((2,)),
            dma((8, 2)), dma((8, 2)), dma((8, 2)), dma((8, 2)), dma((4,)), dma((2,)),
            dma((2, 2, 6)), dma((2, 2, 6)), dma((2, 2, 2)), dma((2, 2)), dma((2, 2)), dma((2, 2)), dma((2,)), dma((2,)),
            dma((2, 4, 2)), dma((2, 4, 2)), dma((2, 4, 2)), dma((2, 4, 2)),
            dma((2, 2)), dma((2, 2)), pltpu.SemaphoreType.REGULAR((7,)),
        ],
        compiler_params=pltpu.CompilerParams(
            collective_id=0, has_side_effects=True, vmem_limit_bytes=60 << 20
        ),
        name="outer_round",
    )(tokens_in[0], cotangent[0], up_weight, down_weight, up_moment, down_moment)


def solution(mesh):
    return jax.shard_map(
        local,
        mesh=mesh,
        in_specs=(
            P("rep", "fsdp", None),
            P("rep", "fsdp", None),
            P(None, "fsdp"),
            P("fsdp", None),
            P("rep", "fsdp"),
            P("fsdp", "rep"),
        ),
        out_specs=(P(None, "fsdp"), P("fsdp", None), P("rep", "fsdp"), P("fsdp", "rep")),
        check_vma=False,
    )
```

```python
import functools

import jax
import jax.numpy as jnp
from jax import lax
from jax.experimental import pallas as pl
from jax.experimental.pallas import tpu as pltpu
from jax.sharding import PartitionSpec as P

inner_rate = 0.3
outer_rate = 0.7
momentum_factor = 0.9

MESH = pl.DeviceIdType.MESH
F32 = jnp.float32
BF16 = jnp.bfloat16

ROWS = 48
SLAB = 4 * ROWS
D = 2048
FL = 256
Q4 = D // 4


def device(x, zhi, core, zlo, y):
    return {"rep": (x * 2 + zhi) * 2 + core, "fsdp": zlo * 4 + y}


def outer_round(
    tok, cot, up, down, mu, md,
    o_up, o_dn, o_mu, o_md,
    X, G, Wu, Wd, accU, accD, dT, aT, sb, rb, ys, yr, cs, cr, cb, zr, us, ds, muv, mdv, W,
    ld, sxz, rxz, sgz, rgz, sxy, rxy, sgy, rgy, sxc, rxc, sgc, rgc, sw, rw,
    sx, rx, sy, ry, sc, rc, sz, rz, sA, rA, sC, rC, sw2, rw2, notes,
):
    rep = lax.axis_index("rep")
    fs = lax.axis_index("fsdp")
    x, zhi, core = rep // 4, (rep // 2) % 2, rep % 2
    zlo, y = fs // 4, fs % 4
    z = zhi * 8 + zlo
    sgn = 1 - 2 * core

    def at_z(zz):
        zz = (zz + 32) % 16
        return device(x, zz // 8, core, zz % 8, y)

    def at_x(xx):
        return device((xx + 8) % 4, zhi, core, zlo, y)

    to_long = at_z(z + sgn)
    to_short = at_z(z - sgn)
    to_pair = device(x, zhi, core, zlo, y + 1 - 2 * (y % 2))
    to_slice = device(x, zhi, core, zlo, 3 - y)
    to_core = device(x, zhi, 1 - core, zlo, y)
    to_cross = device(x, zhi, 1 - core, zlo, 3 - y)
    to_across = at_x(x + 2)
    to_right = at_x(x + 1)
    to_left = at_x(x - 1)
    to_zhi = device(x, 1 - zhi, core, zlo, y)
    home = (y % 2) == core

    def local(src, dst, sem):
        return pltpu.make_async_copy(src, dst, sem)

    def remote(src, dst, ssem, rsem, to):
        return pltpu.make_async_remote_copy(
            src_ref=src, dst_ref=dst, send_sem=ssem, recv_sem=rsem,
            device_id=to, device_id_type=MESH,
        )

    def slot(buf, zi, yi, ci):
        return buf.at[pl.ds(zi * SLAB + (yi * 2 + ci) * ROWS, ROWS), :]

    share_row = pl.multiple_of(rep * 128, 128)
    loads = [
        local(tok, slot(X, 0, 0, 0), ld.at[0]),
        local(cot, slot(G, 0, 0, 0), ld.at[1]),
        local(up.at[pl.ds(share_row, 128), :], us, ld.at[2]),
        local(down.at[:, pl.ds(share_row, 128)], ds, ld.at[3]),
        local(mu, muv, ld.at[4]),
        local(md, mdv, ld.at[5]),
    ]
    for c in loads:
        c.start()

    barrier = pltpu.get_barrier_semaphore()
    everyone = (
        to_long, to_short, to_pair, to_slice, to_core, to_cross, to_right, to_left, to_across,
    )
    for other in everyone:
        pl.semaphore_signal(barrier, inc=1, device_id=other, device_id_type=MESH)
    loads[0].wait()
    loads[1].wait()
    pl.semaphore_wait(barrier, len(everyone))

    def pass_note(k):
        if k > 0:
            pl.semaphore_wait(notes.at[k - 1], 1)
        if k < 7:
            pl.semaphore_signal(notes.at[k], inc=1, device_id=to_long, device_id_type=MESH)

    pass_note(0)

    sent = []

    def go(copy):
        copy.start()
        sent.append(copy)

    def x_z(src_zi, dst_zi, to):
        return remote(slot(X, src_zi, 0, 0), slot(X, dst_zi, 0, 0), sxz.at[dst_zi], rxz.at[dst_zi], to)

    def g_z(src_zi, dst_zi, yi, to):
        return remote(
            slot(G, src_zi, yi, 0), slot(G, dst_zi, yi, 0), sgz.at[dst_zi, yi], rgz.at[dst_zi, yi], to
        )

    def x_y(zi):
        return remote(slot(X, zi, 0, 0), slot(X, zi, 1, 0), sxy.at[zi], rxy.at[zi], to_pair)

    def g_y():
        return remote(slot(G, 0, 0, 0), slot(G, 0, 1, 0), sgy.at[0], rgy.at[0], to_pair)

    def x_c(zi, yi):
        return remote(slot(X, zi, yi, 0), slot(X, zi, yi, 1), sxc.at[zi, yi], rxc.at[zi, yi], to_core)

    def g_c(zi, yi):
        return remote(slot(G, zi, yi, 0), slot(G, zi, yi, 1), sgc.at[zi, yi], rgc.at[zi, yi], to_core)

    go(g_y())
    go(x_z(0, 1, to_long))
    go(x_z(0, 2, to_short))
    go(g_z(0, 1, 0, to_long))
    go(g_z(0, 2, 0, to_short))
    go(x_y(0))
    go(x_c(0, 0))
    go(g_c(0, 0))

    w_send = [
        remote(up, Wu, sw.at[0], rw.at[0], to_slice),
        remote(down, Wd, sw.at[1], rw.at[1], to_slice),
    ]
    w_local = [local(up, Wu, sw.at[2]), local(down, Wd, sw.at[3])]

    @pl.when(home)
    def _():
        for c in w_send + w_local:
            c.start()

    pass_note(1)
    g_y().wait_recv()
    go(g_z(0, 1, 1, to_long))
    go(g_z(0, 2, 1, to_short))
    go(g_c(0, 1))
    x_y(0).wait_recv()
    go(x_c(0, 1))
    pass_note(2)

    def arrived_x(zi, onward, to):
        x_z(0, zi, to_long).wait_recv()
        if onward:
            go(x_z(zi, zi + 2, to))
        go(x_y(zi))
        go(x_c(zi, 0))

    def arrived_g(zi, yi, onward, to):
        g_z(0, zi, yi, to_long).wait_recv()
        if onward:
            go(g_z(zi, zi + 2, yi, to))
        go(g_c(zi, yi))

    def arrived_pair(zi):
        x_y(zi).wait_recv()
        go(x_c(zi, 1))

    def from_core(zi):
        for yi in (0, 1):
            x_c(zi, yi).wait_recv()
            g_c(zi, yi).wait_recv()

    def middle(zi):
        rows = pl.ds(zi * SLAB, SLAB)
        pre = jnp.dot(X[rows, :], Wu[...], preferred_element_type=F32)
        back = lax.dot_general(G[rows, :], Wd[...], (((1,), (1,)), ((), ())), preferred_element_type=F32)
        s = jax.nn.sigmoid(pre)
        act = pre * s
        dpre = back * s * (1.0 + pre * (1.0 - s))
        dT[...] = dpre.astype(BF16).T
        aT[...] = act.astype(BF16).T

    def grads(zi):
        rows = pl.ds(zi * SLAB, SLAB)

        @pl.loop(0, D // 256)
        def _(j):
            cols = pl.ds(pl.multiple_of(j * 256, 256), 256)
            du = jnp.dot(dT[...], X[rows, cols], preferred_element_type=F32)
            dd = jnp.dot(aT[...], G[rows, cols], preferred_element_type=F32)
            accU[:, cols] = du if zi == 0 else accU[:, cols] + du
            accD[:, cols] = dd if zi == 0 else accD[:, cols] + dd

    def unit(zi):
        from_core(zi)
        middle(zi)
        grads(zi)

    for k in (1, 2, 3):
        long, short = 2 * k - 1, 2 * k
        arrived_x(long, True, to_long)
        arrived_x(short, k < 3, to_short)
        if k < 3:
            pass_note(2 * k + 1)
        if k == 3:
            unit(1)
        arrived_g(long, 0, True, to_long)
        arrived_g(short, 0, k < 3, to_short)
        if k == 3:
            unit(2)
        arrived_pair(long)
        arrived_pair(short)
        if k == 3:
            unit(3)
        arrived_g(long, 1, True, to_long)
        arrived_g(short, 1, k < 3, to_short)
        if k < 3:
            pass_note(2 * k + 2)
        else:
            pass_note(7)
        if k == 2:

            @pl.when(home)
            def _():
                for c in w_local:
                    c.wait()

            @pl.when(jnp.logical_not(home))
            def _():
                for c in w_send:
                    c.wait_recv()

            unit(0)
        if k == 3:
            unit(4)

    arrived_x(7, False, to_long)
    unit(5)
    arrived_g(7, 0, False, to_long)
    unit(6)
    arrived_pair(7)
    arrived_g(7, 1, False, to_long)
    from_core(7)
    middle(7)

    last = pl.ds(7 * SLAB, SLAB)
    H4 = Q4 // 2
    HR = FL // 2
    half = (1 - zhi, zhi)

    def hidden(m):
        return pl.ds(m * HR, HR)

    def cols(step, i):
        return pl.ds(pl.multiple_of(((x + step) % 4) * Q4 + half[i] * H4, H4), H4)

    def total_up(m, at):
        return accU[hidden(m), at] + jnp.dot(dT[hidden(m), :], X[last, at], preferred_element_type=F32)

    def total_dn(m, at):
        return accD[hidden(m), at] + jnp.dot(aT[hidden(m), :], G[last, at], preferred_element_type=F32)

    def x_sum(m, i, n):
        return remote(
            sb.at[m, i, n], rb.at[m, i, n], sx.at[m, i, n], rx.at[m, i, n],
            to_right if n % 2 == 0 else to_left,
        )

    def x_first(m, i):
        sb[m, i, 0] = total_up(m, cols(2, i)).astype(BF16)
        go(x_sum(m, i, 0))
        sb[m, i, 1] = total_dn(m, cols(2, i)).astype(BF16)
        go(x_sum(m, i, 1))
        sb[m, i, 2] = total_dn(m, cols(1, i)).astype(BF16)
        go(x_sum(m, i, 2))
        sb[m, i, 3] = total_up(m, cols(3, i)).astype(BF16)
        go(x_sum(m, i, 3))
        for step in (1, 0):
            accU[hidden(m), cols(step, i)] = total_up(m, cols(step, i))
        for step in (3, 0):
            accD[hidden(m), cols(step, i)] = total_dn(m, cols(step, i))

    def x_relay(m, i):
        x_sum(m, i, 0).wait_recv()
        sb[m, i, 4] = (accU[hidden(m), cols(1, i)] + rb[m, i, 0].astype(F32)).astype(BF16)
        go(x_sum(m, i, 4))
        x_sum(m, i, 1).wait_recv()
        sb[m, i, 5] = (accD[hidden(m), cols(3, i)] + rb[m, i, 1].astype(F32)).astype(BF16)
        go(x_sum(m, i, 5))

    def part(m, i, a, off, width):
        at = pl.ds(pl.multiple_of(x * Q4 + half[i] * H4 + off, 128), width)
        here = pl.ds(pl.multiple_of(off, 128), width)
        if a == 0:
            return accU[hidden(m), at] + rb[m, i, 3, :, here].astype(F32) + rb[m, i, 4, :, here].astype(F32)
        return accD[hidden(m), at] + rb[m, i, 2, :, here].astype(F32) + rb[m, i, 5, :, here].astype(F32)

    def y_home(m, i):
        return remote(ys.at[m, i, 0], yr.at[m, i], sy.at[m, i, 0], ry.at[m, i], to_slice)

    def y_cross(m, i):
        return remote(ys.at[m, i, 1], yr.at[m, i], sy.at[m, i, 1], ry.at[m, i], to_cross)

    def c_sum(m, i):
        return remote(cs.at[m, i], cr.at[m, i], sc.at[m, i], rc.at[m, i], to_core)

    mine = pl.multiple_of(core * 128, 128)
    theirs = pl.multiple_of((1 - core) * 128, 128)

    def y_out(m, i):
        for n in (2, 3, 4, 5):
            x_sum(m, i, n).wait_recv()

        @pl.when(jnp.logical_not(home))
        def _():
            for a in (0, 1):
                ys[m, i, 0, a] = part(m, i, a, mine, 128).astype(BF16)
            y_home(m, i).start()
            for a in (0, 1):
                ys[m, i, 1, a] = part(m, i, a, theirs, 128).astype(BF16)
            y_cross(m, i).start()

        @pl.when(home)
        def _():
            for a in (0, 1):
                cs[m, i, a] = part(m, i, a, theirs, 128).astype(BF16)
            c_sum(m, i).start()

    def y_in(m, i):
        @pl.when(jnp.logical_not(home))
        def _():
            c_sum(m, i).wait_recv()
            y_cross(m, i).wait_recv()
            for a in (0, 1):
                cb[m, i, a] = (cr[m, i, a].astype(F32) + yr[m, i, a].astype(F32)).astype(BF16)

        @pl.when(home)
        def _():
            y_home(m, i).wait_recv()
            for a in (0, 1):
                cb[m, i, a] = (part(m, i, a, mine, 128) + yr[m, i, a].astype(F32)).astype(BF16)

    def z_sum(m):
        return remote(cb.at[m, 0], zr.at[m], sz.at[m], rz.at[m], to_zhi)

    last_z = []

    def outer_step(m):
        scale = inner_rate / 16
        z_sum(m).wait_recv()
        mean = (cb[m, 1, 0].astype(F32) + zr[m, 0].astype(F32)).T * scale
        moment = momentum_factor * muv[:, hidden(m)] + mean
        o_mu[:, hidden(m)] = moment
        W[rep, m, 0] = (
            us[:, hidden(m)].astype(F32) - outer_rate * (mean + momentum_factor * moment)
        ).astype(BF16)
        last_z.append(a_z(0, m))
        last_z[-1].start()
        mean = (cb[m, 1, 1].astype(F32) + zr[m, 1].astype(F32)) * scale
        moment = momentum_factor * mdv[hidden(m), :] + mean
        o_md[hidden(m), :] = moment
        W[rep, m, 1] = (
            ds[hidden(m), :].astype(F32) - outer_rate * (mean + momentum_factor * moment)
        ).astype(BF16)
        last_z.append(a_z(1, m))
        last_z[-1].start()
        x_out(0, m)

    back_by = {0: 0, 1: 1, 2: 2, 3: -1}

    def share(q, j, cc):
        return (((x - back_by[j] + 4) % 4) * 2 + (zhi + q) % 2) * 2 + cc

    def a_z(a, m):
        block = W.at[rep, m, a]
        return remote(block, block, sw2.at[m, a], rw2.at[m, a], to_zhi)

    def z_in(a, m):
        block = W.at[share(1, 0, core), m, a]
        return remote(block, block, sw2.at[m, a], rw2.at[m, a], to_zhi)

    def a_x(m, q, dst_j, to):
        block = W.at[share(q, 0, core), m]
        return remote(block, block, sA.at[q, dst_j, m], rA.at[q, dst_j, m], to)

    def x_in(m, q, j):
        block = W.at[share(q, j, core), m]
        return remote(block, block, sA.at[q, j, m], rA.at[q, j, m], to_right)

    def a_c(m, q, j):
        block = W.at[share(q, j, core), m]
        return remote(block, block, sC.at[q, j, m], rC.at[q, j, m], to_core)

    def c_in(m, q, j):
        block = W.at[share(q, j, 1 - core), m]
        return remote(block, block, sC.at[q, j, m], rC.at[q, j, m], to_core)

    def place(m, q, j, cc):
        r = share(q, j, cc)
        at = pl.ds(pl.multiple_of(r * 128, 128), 128)
        o_up[at, hidden(m)] = W[r, m, 0]
        o_dn[hidden(m), at] = W[r, m, 1]

    def x_out(q, m):
        if q == 1:
            z_in(0, m).wait_recv()
            z_in(1, m).wait_recv()
        go(a_x(m, q, 2, to_across))
        go(a_x(m, q, 1, to_right))
        go(a_x(m, q, 3, to_left))
        go(a_c(m, q, 0))

    def x_pass(q, m):
        place(m, q, 0, core)
        for j in (1, 3, 2):
            x_in(m, q, j).wait_recv()
            go(a_c(m, q, j))
            place(m, q, j, core)

    def from_other(q, m):
        for j in (0, 1, 3, 2):
            c_in(m, q, j).wait_recv()
            place(m, q, j, 1 - core)

    def settle(copies):
        for c in copies:
            c.wait_send()

    x_first(0, 0)
    x_relay(0, 0)
    x_first(1, 0)
    y_out(0, 0)
    x_relay(1, 0)
    x_first(0, 1)
    y_in(0, 0)
    go(z_sum(0))
    y_out(1, 0)
    x_relay(0, 1)
    x_first(1, 1)
    y_in(1, 0)
    go(z_sum(1))
    y_out(0, 1)
    x_relay(1, 1)
    y_in(0, 1)
    y_out(1, 1)
    for c in loads[2:]:
        c.wait()
    early = list(sent)
    sent.clear()
    outer_step(0)
    y_in(1, 1)
    x_pass(0, 0)

    outer_step(1)
    settle(early)

    @pl.when(home)
    def _():
        for c in w_send:
            c.wait_send()
        for m in (0, 1):
            for i in (0, 1):
                c_sum(m, i).wait_send()

    @pl.when(jnp.logical_not(home))
    def _():
        for m in (0, 1):
            for i in (0, 1):
                y_home(m, i).wait_send()
                y_cross(m, i).wait_send()

    from_other(0, 0)
    x_out(1, 0)
    x_pass(0, 1)
    x_pass(1, 0)
    from_other(0, 1)
    settle(sent)
    sent.clear()
    x_out(1, 1)
    from_other(1, 0)
    x_pass(1, 1)
    from_other(1, 1)
    settle(sent + last_z)


def local(tokens_in, cotangent, up_weight, down_weight, up_moment, down_moment):
    dma = pltpu.SemaphoreType.DMA
    vmem = pltpu.VMEM
    return pl.pallas_call(
        outer_round,
        out_shape=(
            jax.ShapeDtypeStruct(up_weight.shape, BF16),
            jax.ShapeDtypeStruct(down_weight.shape, BF16),
            jax.ShapeDtypeStruct(up_moment.shape, F32),
            jax.ShapeDtypeStruct(down_moment.shape, F32),
        ),
        in_specs=[pl.BlockSpec(memory_space=pltpu.HBM)] * 6,
        out_specs=[pl.BlockSpec(memory_space=pltpu.VMEM)] * 4,
        scratch_shapes=[
            vmem((8 * SLAB, D), BF16), vmem((8 * SLAB, D), BF16),
            vmem((D, FL), BF16), vmem((FL, D), BF16),
            vmem((FL, D), F32), vmem((FL, D), F32),
            vmem((FL, SLAB), BF16), vmem((FL, SLAB), BF16),
            vmem((2, 2, 6, FL // 2, Q4 // 2), BF16), vmem((2, 2, 6, FL // 2, Q4 // 2), BF16),
            vmem((2, 2, 2, 2, FL // 2, 128), BF16), vmem((2, 2, 2, FL // 2, 128), BF16),
            vmem((2, 2, 2, FL // 2, 128), BF16), vmem((2, 2, 2, FL // 2, 128), BF16),
            vmem((2, 2, 2, FL // 2, 128), BF16),
            vmem((2, 2, FL // 2, 128), BF16),
            vmem((128, FL), BF16), vmem((FL, 128), BF16),
            vmem((128, FL), F32), vmem((FL, 128), F32),
            vmem((16, 2, 2, FL // 2, 128), BF16),
            dma((6,)),
            dma((8,)), dma((8,)), dma((8, 2)), dma((8, 2)), dma((8,)), dma((8,)), dma((1,)), dma((1,)),
            dma((8, 2)), dma((8, 2)), dma((8, 2)), dma((8, 2)), dma((4,)), dma((2,)),
            dma((2, 2, 6)), dma((2, 2, 6)), dma((2, 2, 2)), dma((2, 2)), dma((2, 2)), dma((2, 2)), dma((2,)), dma((2,)),
            dma((2, 4, 2)), dma((2, 4, 2)), dma((2, 4, 2)), dma((2, 4, 2)),
            dma((2, 2)), dma((2, 2)), pltpu.SemaphoreType.REGULAR((7,)),
        ],
        compiler_params=pltpu.CompilerParams(
            collective_id=0, has_side_effects=True, vmem_limit_bytes=60 << 20
        ),
        name="outer_round",
    )(tokens_in[0], cotangent[0], up_weight, down_weight, up_moment, down_moment)


def solution(mesh):
    return jax.shard_map(
        local,
        mesh=mesh,
        in_specs=(
            P("rep", "fsdp", None),
            P("rep", "fsdp", None),
            P(None, "fsdp"),
            P("fsdp", None),
            P("rep", "fsdp"),
            P("fsdp", "rep"),
        ),
        out_specs=(P(None, "fsdp"), P("fsdp", None), P("rep", "fsdp"), P("fsdp", "rep")),
        check_vma=False,
    )
```

```python
import functools

import jax
import jax.numpy as jnp
from jax import lax
from jax.experimental import pallas as pl
from jax.experimental.pallas import tpu as pltpu
from jax.sharding import PartitionSpec as P

inner_rate = 0.3
outer_rate = 0.7
momentum_factor = 0.9

MESH = pl.DeviceIdType.MESH
F32 = jnp.float32
BF16 = jnp.bfloat16

ROWS = 48
SLAB = 4 * ROWS
D = 2048
FL = 256
Q4 = D // 4


def device(x, zhi, core, zlo, y):
    return {"rep": (x * 2 + zhi) * 2 + core, "fsdp": zlo * 4 + y}


def outer_round(
    tok, cot, up, down, mu, md,
    o_up, o_dn, o_mu, o_md,
    X, G, Wu, Wd, accU, accD, dT, aT, sb, rb, ys, yr, cs, cr, cb, zr, us, ds, muv, mdv, W,
    ld, sxz, rxz, sgz, rgz, sxy, rxy, sgy, rgy, sxc, rxc, sgc, rgc, sw, rw,
    sx, rx, sy, ry, sc, rc, sz, rz, sA, rA, sC, rC, notes,
):
    rep = lax.axis_index("rep")
    fs = lax.axis_index("fsdp")
    x, zhi, core = rep // 4, (rep // 2) % 2, rep % 2
    zlo, y = fs // 4, fs % 4
    z = zhi * 8 + zlo
    sgn = 1 - 2 * core

    def at_z(zz):
        zz = (zz + 32) % 16
        return device(x, zz // 8, core, zz % 8, y)

    def at_x(xx):
        return device((xx + 8) % 4, zhi, core, zlo, y)

    to_long = at_z(z + sgn)
    to_short = at_z(z - sgn)
    to_pair = device(x, zhi, core, zlo, y + 1 - 2 * (y % 2))
    to_slice = device(x, zhi, core, zlo, 3 - y)
    to_core = device(x, zhi, 1 - core, zlo, y)
    to_cross = device(x, zhi, 1 - core, zlo, 3 - y)
    to_across = at_x(x + 2)
    to_right = at_x(x + 1)
    to_left = at_x(x - 1)
    to_zhi = device(x, 1 - zhi, core, zlo, y)
    home = (y % 2) == core

    def local(src, dst, sem):
        return pltpu.make_async_copy(src, dst, sem)

    def remote(src, dst, ssem, rsem, to):
        return pltpu.make_async_remote_copy(
            src_ref=src, dst_ref=dst, send_sem=ssem, recv_sem=rsem,
            device_id=to, device_id_type=MESH,
        )

    def slot(buf, zi, yi, ci):
        return buf.at[pl.ds(zi * SLAB + (yi * 2 + ci) * ROWS, ROWS), :]

    share_row = pl.multiple_of(rep * 128, 128)
    loads = [
        local(tok, slot(X, 0, 0, 0), ld.at[0]),
        local(cot, slot(G, 0, 0, 0), ld.at[1]),
        local(up.at[pl.ds(share_row, 128), :], us, ld.at[2]),
        local(down.at[:, pl.ds(share_row, 128)], ds, ld.at[3]),
        local(mu, muv, ld.at[4]),
        local(md, mdv, ld.at[5]),
    ]
    for c in loads:
        c.start()

    barrier = pltpu.get_barrier_semaphore()
    everyone = (
        to_long, to_short, to_pair, to_slice, to_core, to_cross, to_right, to_left, to_across,
    )
    for other in everyone:
        pl.semaphore_signal(barrier, inc=1, device_id=other, device_id_type=MESH)
    loads[0].wait()
    loads[1].wait()
    pl.semaphore_wait(barrier, len(everyone))

    def pass_note(k):
        if k > 0:
            pl.semaphore_wait(notes.at[k - 1], 1)
        if k < 7:
            pl.semaphore_signal(notes.at[k], inc=1, device_id=to_long, device_id_type=MESH)

    pass_note(0)

    sent = []

    def go(copy):
        copy.start()
        sent.append(copy)

    def x_z(src_zi, dst_zi, to):
        return remote(slot(X, src_zi, 0, 0), slot(X, dst_zi, 0, 0), sxz.at[dst_zi], rxz.at[dst_zi], to)

    def g_z(src_zi, dst_zi, yi, to):
        return remote(
            slot(G, src_zi, yi, 0), slot(G, dst_zi, yi, 0), sgz.at[dst_zi, yi], rgz.at[dst_zi, yi], to
        )

    def x_y(zi):
        return remote(slot(X, zi, 0, 0), slot(X, zi, 1, 0), sxy.at[zi], rxy.at[zi], to_pair)

    def g_y():
        return remote(slot(G, 0, 0, 0), slot(G, 0, 1, 0), sgy.at[0], rgy.at[0], to_pair)

    def x_c(zi, yi):
        return remote(slot(X, zi, yi, 0), slot(X, zi, yi, 1), sxc.at[zi, yi], rxc.at[zi, yi], to_core)

    def g_c(zi, yi):
        return remote(slot(G, zi, yi, 0), slot(G, zi, yi, 1), sgc.at[zi, yi], rgc.at[zi, yi], to_core)

    go(g_y())
    go(x_z(0, 1, to_long))
    go(x_z(0, 2, to_short))
    go(g_z(0, 1, 0, to_long))
    go(g_z(0, 2, 0, to_short))
    go(x_y(0))
    go(x_c(0, 0))
    go(g_c(0, 0))

    w_send = [
        remote(up, Wu, sw.at[0], rw.at[0], to_slice),
        remote(down, Wd, sw.at[1], rw.at[1], to_slice),
    ]
    w_local = [local(up, Wu, sw.at[2]), local(down, Wd, sw.at[3])]

    @pl.when(home)
    def _():
        for c in w_send + w_local:
            c.start()

    pass_note(1)
    g_y().wait_recv()
    go(g_z(0, 1, 1, to_long))
    go(g_z(0, 2, 1, to_short))
    go(g_c(0, 1))
    x_y(0).wait_recv()
    go(x_c(0, 1))
    pass_note(2)

    def arrived_x(zi, onward, to):
        x_z(0, zi, to_long).wait_recv()
        if onward:
            go(x_z(zi, zi + 2, to))
        go(x_y(zi))
        go(x_c(zi, 0))

    def arrived_g(zi, yi, onward, to):
        g_z(0, zi, yi, to_long).wait_recv()
        if onward:
            go(g_z(zi, zi + 2, yi, to))
        go(g_c(zi, yi))

    def arrived_pair(zi):
        x_y(zi).wait_recv()
        go(x_c(zi, 1))

    def from_core(zi):
        for yi in (0, 1):
            x_c(zi, yi).wait_recv()
            g_c(zi, yi).wait_recv()

    def middle(zi, n):
        rows = pl.ds(zi * SLAB, n * SLAB)
        pre = jnp.dot(X[rows, :], Wu[...], preferred_element_type=F32)
        back = lax.dot_general(G[rows, :], Wd[...], (((1,), (1,)), ((), ())), preferred_element_type=F32)
        s = jax.nn.sigmoid(pre)
        act = pre * s
        dpre = back * s * (1.0 + pre * (1.0 - s))
        dT[:, : n * SLAB] = dpre.astype(BF16).T
        aT[:, : n * SLAB] = act.astype(BF16).T

    def grads(zi, n):
        rows = pl.ds(zi * SLAB, n * SLAB)

        @pl.loop(0, D // 256)
        def _(j):
            cols = pl.ds(pl.multiple_of(j * 256, 256), 256)
            du = jnp.dot(dT[:, : n * SLAB], X[rows, cols], preferred_element_type=F32)
            dd = jnp.dot(aT[:, : n * SLAB], G[rows, cols], preferred_element_type=F32)
            accU[:, cols] = du if zi == 0 else accU[:, cols] + du
            accD[:, cols] = dd if zi == 0 else accD[:, cols] + dd

    def unit(zi, n):
        for i in range(n):
            from_core(zi + i)
        middle(zi, n)
        grads(zi, n)

    for k in (1, 2, 3):
        long, short = 2 * k - 1, 2 * k
        arrived_x(long, True, to_long)
        arrived_x(short, k < 3, to_short)
        if k < 3:
            pass_note(2 * k + 1)
        if k == 3:
            unit(1, 2)
        arrived_g(long, 0, True, to_long)
        arrived_g(short, 0, k < 3, to_short)
        arrived_pair(long)
        arrived_pair(short)
        if k == 3:
            unit(3, 2)
        arrived_g(long, 1, True, to_long)
        arrived_g(short, 1, k < 3, to_short)
        if k < 3:
            pass_note(2 * k + 2)
        else:
            pass_note(7)
        if k == 2:

            @pl.when(home)
            def _():
                for c in w_local:
                    c.wait()

            @pl.when(jnp.logical_not(home))
            def _():
                for c in w_send:
                    c.wait_recv()

            unit(0, 1)

    arrived_x(7, False, to_long)
    arrived_g(7, 0, False, to_long)
    unit(5, 2)
    arrived_pair(7)
    arrived_g(7, 1, False, to_long)
    from_core(7)
    middle(7, 1)

    last = pl.ds(7 * SLAB, SLAB)
    H4 = Q4 // 2
    HR = FL // 2
    half = (1 - zhi, zhi)

    def hidden(m):
        return pl.ds(m * HR, HR)

    def cols(step, i):
        return pl.ds(pl.multiple_of(((x + step) % 4) * Q4 + half[i] * H4, H4), H4)

    def total_up(m, at):
        return accU[hidden(m), at] + jnp.dot(dT[hidden(m), :SLAB], X[last, at], preferred_element_type=F32)

    def total_dn(m, at):
        return accD[hidden(m), at] + jnp.dot(aT[hidden(m), :SLAB], G[last, at], preferred_element_type=F32)

    def x_sum(m, i, n):
        return remote(
            sb.at[m, i, n], rb.at[m, i, n], sx.at[m, i, n], rx.at[m, i, n],
            to_right if n % 2 == 0 else to_left,
        )

    def x_first(m, i):
        sb[m, i, 0] = total_up(m, cols(2, i)).astype(BF16)
        go(x_sum(m, i, 0))
        sb[m, i, 1] = total_dn(m, cols(2, i)).astype(BF16)
        go(x_sum(m, i, 1))
        sb[m, i, 2] = total_dn(m, cols(1, i)).astype(BF16)
        go(x_sum(m, i, 2))
        sb[m, i, 3] = total_up(m, cols(3, i)).astype(BF16)
        go(x_sum(m, i, 3))
        for step in (1, 0):
            accU[hidden(m), cols(step, i)] = total_up(m, cols(step, i))
        for step in (3, 0):
            accD[hidden(m), cols(step, i)] = total_dn(m, cols(step, i))

    def x_relay(m, i):
        x_sum(m, i, 0).wait_recv()
        sb[m, i, 4] = (accU[hidden(m), cols(1, i)] + rb[m, i, 0].astype(F32)).astype(BF16)
        go(x_sum(m, i, 4))
        x_sum(m, i, 1).wait_recv()
        sb[m, i, 5] = (accD[hidden(m), cols(3, i)] + rb[m, i, 1].astype(F32)).astype(BF16)
        go(x_sum(m, i, 5))

    def part(m, i, a, off, width):
        at = pl.ds(pl.multiple_of(x * Q4 + half[i] * H4 + off, 128), width)
        here = pl.ds(pl.multiple_of(off, 128), width)
        if a == 0:
            return accU[hidden(m), at] + rb[m, i, 3, :, here].astype(F32) + rb[m, i, 4, :, here].astype(F32)
        return accD[hidden(m), at] + rb[m, i, 2, :, here].astype(F32) + rb[m, i, 5, :, here].astype(F32)

    def y_home(m, i):
        return remote(ys.at[m, i, 0], yr.at[m, i], sy.at[m, i, 0], ry.at[m, i], to_slice)

    def y_cross(m, i):
        return remote(ys.at[m, i, 1], yr.at[m, i], sy.at[m, i, 1], ry.at[m, i], to_cross)

    def c_sum(m, i):
        return remote(cs.at[m, i], cr.at[m, i], sc.at[m, i], rc.at[m, i], to_core)

    mine = pl.multiple_of(core * 128, 128)
    theirs = pl.multiple_of((1 - core) * 128, 128)

    def y_out(m, i):
        for n in (2, 3, 4, 5):
            x_sum(m, i, n).wait_recv()

        @pl.when(jnp.logical_not(home))
        def _():
            for a in (0, 1):
                ys[m, i, 0, a] = part(m, i, a, mine, 128).astype(BF16)
            y_home(m, i).start()
            for a in (0, 1):
                ys[m, i, 1, a] = part(m, i, a, theirs, 128).astype(BF16)
            y_cross(m, i).start()

        @pl.when(home)
        def _():
            for a in (0, 1):
                cs[m, i, a] = part(m, i, a, theirs, 128).astype(BF16)
            c_sum(m, i).start()

    def y_in(m, i):
        @pl.when(jnp.logical_not(home))
        def _():
            c_sum(m, i).wait_recv()
            y_cross(m, i).wait_recv()
            for a in (0, 1):
                cb[m, i, a] = (cr[m, i, a].astype(F32) + yr[m, i, a].astype(F32)).astype(BF16)

        @pl.when(home)
        def _():
            y_home(m, i).wait_recv()
            for a in (0, 1):
                cb[m, i, a] = (part(m, i, a, mine, 128) + yr[m, i, a].astype(F32)).astype(BF16)

    def z_sum(m):
        return remote(cb.at[m, 0], zr.at[m], sz.at[m], rz.at[m], to_zhi)

    def outer_step(m):
        scale = inner_rate / 16
        z_sum(m).wait_recv()
        mean = (cb[m, 1, 0].astype(F32) + zr[m, 0].astype(F32)).T * scale
        moment = momentum_factor * muv[:, hidden(m)] + mean
        o_mu[:, hidden(m)] = moment
        W[rep, m, 0] = (
            us[:, hidden(m)].astype(F32) - outer_rate * (mean + momentum_factor * moment)
        ).astype(BF16)
        mean = (cb[m, 1, 1].astype(F32) + zr[m, 1].astype(F32)) * scale
        moment = momentum_factor * mdv[hidden(m), :] + mean
        o_md[hidden(m), :] = moment
        W[rep, m, 1] = (
            ds[hidden(m), :].astype(F32) - outer_rate * (mean + momentum_factor * moment)
        ).astype(BF16)
        go(a_z(m))
        x_out(0, m)

    back_by = {0: 0, 1: 1, 2: 2, 3: -1}

    def share(q, j, cc):
        return (((x - back_by[j] + 4) % 4) * 2 + (zhi + q) % 2) * 2 + cc

    def a_z(m):
        block = W.at[rep, m]
        return remote(block, block, sA.at[1, 0, m], rA.at[1, 0, m], to_zhi)

    def z_in(m):
        block = W.at[share(1, 0, core), m]
        return remote(block, block, sA.at[1, 0, m], rA.at[1, 0, m], to_zhi)

    def a_x(m, q, dst_j, to):
        block = W.at[share(q, 0, core), m]
        return remote(block, block, sA.at[q, dst_j, m], rA.at[q, dst_j, m], to)

    def x_in(m, q, j):
        block = W.at[share(q, j, core), m]
        return remote(block, block, sA.at[q, j, m], rA.at[q, j, m], to_right)

    def a_c(m, q, j):
        block = W.at[share(q, j, core), m]
        return remote(block, block, sC.at[q, j, m], rC.at[q, j, m], to_core)

    def c_in(m, q, j):
        block = W.at[share(q, j, 1 - core), m]
        return remote(block, block, sC.at[q, j, m], rC.at[q, j, m], to_core)

    def place(m, q, j, cc):
        r = share(q, j, cc)
        at = pl.ds(pl.multiple_of(r * 128, 128), 128)
        o_up[at, hidden(m)] = W[r, m, 0]
        o_dn[hidden(m), at] = W[r, m, 1]

    def x_out(q, m):
        if q == 1:
            z_in(m).wait_recv()
        go(a_x(m, q, 2, to_across))
        go(a_x(m, q, 1, to_right))
        go(a_x(m, q, 3, to_left))
        go(a_c(m, q, 0))

    def x_pass(q, m):
        place(m, q, 0, core)
        for j in (1, 3, 2):
            x_in(m, q, j).wait_recv()
            go(a_c(m, q, j))
            place(m, q, j, core)

    def from_other(q, m):
        for j in (0, 1, 3, 2):
            c_in(m, q, j).wait_recv()
            place(m, q, j, 1 - core)

    def settle(copies):
        for c in copies:
            c.wait_send()

    x_first(0, 0)
    x_relay(0, 0)
    x_first(1, 0)
    y_out(0, 0)
    x_relay(1, 0)
    x_first(0, 1)
    y_in(0, 0)
    go(z_sum(0))
    y_out(1, 0)
    x_relay(0, 1)
    x_first(1, 1)
    y_in(1, 0)
    go(z_sum(1))
    y_out(0, 1)
    x_relay(1, 1)
    y_in(0, 1)
    y_out(1, 1)
    for c in loads[2:]:
        c.wait()
    early = list(sent)
    sent.clear()
    outer_step(0)
    y_in(1, 1)
    x_pass(0, 0)

    outer_step(1)
    settle(early)

    @pl.when(home)
    def _():
        for c in w_send:
            c.wait_send()
        for m in (0, 1):
            for i in (0, 1):
                c_sum(m, i).wait_send()

    @pl.when(jnp.logical_not(home))
    def _():
        for m in (0, 1):
            for i in (0, 1):
                y_home(m, i).wait_send()
                y_cross(m, i).wait_send()

    from_other(0, 0)
    x_out(1, 0)
    x_pass(0, 1)
    x_pass(1, 0)
    from_other(0, 1)
    x_out(1, 1)
    from_other(1, 0)
    x_pass(1, 1)
    from_other(1, 1)
    settle(sent)


def local(tokens_in, cotangent, up_weight, down_weight, up_moment, down_moment):
    dma = pltpu.SemaphoreType.DMA
    vmem = pltpu.VMEM
    return pl.pallas_call(
        outer_round,
        out_shape=(
            jax.ShapeDtypeStruct(up_weight.shape, BF16),
            jax.ShapeDtypeStruct(down_weight.shape, BF16),
            jax.ShapeDtypeStruct(up_moment.shape, F32),
            jax.ShapeDtypeStruct(down_moment.shape, F32),
        ),
        in_specs=[pl.BlockSpec(memory_space=pltpu.HBM)] * 6,
        out_specs=[pl.BlockSpec(memory_space=pltpu.VMEM)] * 4,
        scratch_shapes=[
            vmem((8 * SLAB, D), BF16), vmem((8 * SLAB, D), BF16),
            vmem((D, FL), BF16), vmem((FL, D), BF16),
            vmem((FL, D), F32), vmem((FL, D), F32),
            vmem((FL, 2 * SLAB), BF16), vmem((FL, 2 * SLAB), BF16),
            vmem((2, 2, 6, FL // 2, Q4 // 2), BF16), vmem((2, 2, 6, FL // 2, Q4 // 2), BF16),
            vmem((2, 2, 2, 2, FL // 2, 128), BF16), vmem((2, 2, 2, FL // 2, 128), BF16),
            vmem((2, 2, 2, FL // 2, 128), BF16), vmem((2, 2, 2, FL // 2, 128), BF16),
            vmem((2, 2, 2, FL // 2, 128), BF16),
            vmem((2, 2, FL // 2, 128), BF16),
            vmem((128, FL), BF16), vmem((FL, 128), BF16),
            vmem((128, FL), F32), vmem((FL, 128), F32),
            vmem((16, 2, 2, FL // 2, 128), BF16),
            dma((6,)),
            dma((8,)), dma((8,)), dma((8, 2)), dma((8, 2)), dma((8,)), dma((8,)), dma((1,)), dma((1,)),
            dma((8, 2)), dma((8, 2)), dma((8, 2)), dma((8, 2)), dma((4,)), dma((2,)),
            dma((2, 2, 6)), dma((2, 2, 6)), dma((2, 2, 2)), dma((2, 2)), dma((2, 2)), dma((2, 2)), dma((2,)), dma((2,)),
            dma((2, 4, 2)), dma((2, 4, 2)), dma((2, 4, 2)), dma((2, 4, 2)),
            pltpu.SemaphoreType.REGULAR((7,)),
        ],
        compiler_params=pltpu.CompilerParams(
            collective_id=0, has_side_effects=True, vmem_limit_bytes=60 << 20
        ),
        name="outer_round",
    )(tokens_in[0], cotangent[0], up_weight, down_weight, up_moment, down_moment)


def solution(mesh):
    return jax.shard_map(
        local,
        mesh=mesh,
        in_specs=(
            P("rep", "fsdp", None),
            P("rep", "fsdp", None),
            P(None, "fsdp"),
            P("fsdp", None),
            P("rep", "fsdp"),
            P("fsdp", "rep"),
        ),
        out_specs=(P(None, "fsdp"), P("fsdp", None), P("rep", "fsdp"), P("fsdp", "rep")),
        check_vma=False,
    )
```
